256 devices in a mesh: ctx: 32 (over y, z), tp: 8 (over x, core).
Axes of the slice: x: 4, y: 4, z: 8, core: 2. Of those that a mesh axis runs over, the one named last changes fastest.
Arguments:
- hidden: bfloat16 [512, 8192], P('ctx')
- weight: bfloat16 [8192, 98304], P(None, ('ctx', 'tp'))
- targets: int32 [512], replicated, may hold values from 0 to 98303
- row_seq: int32 [512], replicated, may hold values from 0 to 1, as said below
- ref_logp: float32 [2], replicated, may hold values from -120 to 120
Outputs:
- dpo_loss: float32 [], replicated
- d_hidden: bfloat16 [512, 8192], P('ctx', 'tp')
- d_weight: bfloat16 [8192, 98304], P(None, ('ctx', 'tp'))
The draws below stay inside these ranges and needn't reach their ends.
Inputs may be any that keep to these rules, and one draw needn't show every extreme that they name: `row_seq`: each of 0 and 1 names exactly 256 rows.
All inputs are finite; a program needn't handle non-finite values.
Results may differ from the reference program's by a relative error of at most 0.023.
Values may be sent and summed in bfloat16 or wider, within the bound.
A program may use at most 128 MiB of HBM per device.

```python
import math
import jax
import jax.numpy as jnp
import numpy as np
from jax import lax

D = 8192
VOCAB = 98304
RESP = 256
SEQS = 2
ROWS = 512


def column_normals(key, columns):
    return jax.vmap(lambda column: jnp.clip(jax.random.normal(jax.random.fold_in(key, column), (D,), jnp.float32), -6.0, 6.0))(columns)


def draw_weight(key, part):
    base_rows = column_normals(key, jnp.arange(VOCAB, dtype=jnp.int32))
    return (base_rows.T * (3.0 / math.sqrt(D))).astype(jnp.bfloat16)


def draw_hidden(key, part):
    base_key = key
    key = jax.random.fold_in(key, 5)
    keys = jax.random.split(key, 7)
    values = jnp.clip(jax.random.normal(keys[0], (ROWS, D), jnp.float32), -6.0, 6.0)
    chosen_rows = jax.random.randint(keys[2], (8,), 0, ROWS)
    first_cols = jax.random.randint(keys[3], (8,), 0, VOCAB)
    second_cols = jax.random.randint(keys[4], (8,), 0, VOCAB)
    strength = jax.random.uniform(keys[5], (8,), jnp.float32, 0.4, 1.0)
    spacing = jax.random.uniform(keys[6], (8,), jnp.float32, 1.0, 3.0) / 300.0
    factor = 100.0 / math.sqrt(D)
    aligned = factor * (strength[:, None] * column_normals(base_key, first_cols) + (strength - spacing)[:, None] * column_normals(base_key, second_cols))
    values = values.at[chosen_rows].set(aligned)
    return values.astype(jnp.bfloat16)


def draw_row_seq(key, part):
    key = jax.random.fold_in(key, 7)
    order = jax.random.permutation(key, ROWS)
    return (order >= RESP).astype(jnp.int32)


def touch_ends(drawn, rng, low, largest):
    spot = [jax.random.randint(jax.random.fold_in(rng, axis), (), 0, length) for axis, length in enumerate(drawn.shape)]
    main_axis = drawn.shape.index(max(drawn.shape))
    next_to = spot[:main_axis] + [(spot[main_axis] + 1) % drawn.shape[main_axis]] + spot[main_axis + 1:]
    return drawn.at[tuple(spot)].set(low).at[tuple(next_to)].set(largest)


def wide_ids(rng, extent, amount, lean):
    loads = [min(1 << octave, amount + 1 - (1 << octave)) * (1 << 20) // math.isqrt((1 << octave) ** lean) + 1 for octave in range((amount + 1).bit_length()) if 1 << octave <= amount]
    spread = 1 + sum(loads) // (1 << 30)
    grid = np.cumsum(np.array([max(1, weight // spread) for weight in loads]))
    ticket = jax.random.randint(jax.random.fold_in(rng, 1), extent, 0, int(grid[len(loads) - 1]))
    start = jnp.left_shift(1, jnp.searchsorted(jnp.asarray(grid, jnp.int32), ticket, side="right").astype(jnp.int32))
    grade = start - 1 + jax.random.randint(jax.random.fold_in(rng, 4), extent, 0, 1 << 30) % jnp.minimum(start, amount + 1 - start)
    return jax.random.permutation(jax.random.fold_in(rng, 2), amount)[grade].astype(jnp.int32)


def bell_draw(stream_key, extent, deviation, limit, held_as=jnp.bfloat16):
    array = deviation * jax.random.normal(stream_key, extent, jnp.float32)
    return jnp.clip(array, min=-limit, max=limit).astype(held_as)


def setup_inputs(seed: int = 0) -> dict:
    key_list = jax.random.split(jax.random.key(seed), 6)
    hidden = draw_hidden(jax.random.fold_in(key_list[5], 71), 0)
    weight = draw_weight(jax.random.fold_in(key_list[5], 71), 0)
    targets = touch_ends(wide_ids(key_list[2], (ROWS,), VOCAB, 2), jax.random.fold_in(key_list[2], 3), 0, VOCAB - 1).astype(jnp.int32)
    row_seq = draw_row_seq(jax.random.fold_in(key_list[5], 71), 0)
    ref_logp = bell_draw(key_list[4], (SEQS,), 20.0, 120.0, jnp.float32)
    return dict(hidden=hidden, weight=weight, targets=targets, row_seq=row_seq, ref_logp=ref_logp)


DPO_BETA = 0.01
LOSS_SCALE = 1024.0


def reference(hidden, weight, targets, row_seq, ref_logp):
    logits = jnp.dot(hidden, weight, preferred_element_type=jnp.float32)
    row_peak = jnp.max(logits, axis=1)
    row_total = jnp.sum(jnp.exp(logits - row_peak[:, None]), axis=1)
    lse = row_peak + jnp.log(row_total)
    columns = jnp.arange(VOCAB, dtype=jnp.int32)
    matches = columns[None, :] == targets[:, None]
    picked = jnp.sum(jnp.where(matches, logits, jnp.float32(0.0)), axis=1)
    row_logp = picked - lse
    member = (row_seq[:, None] == jnp.arange(SEQS, dtype=jnp.int32)[None, :]).astype(jnp.float32)
    seq_logp = jnp.sum(member * row_logp[:, None], axis=0)
    margin = DPO_BETA * ((seq_logp[0] - ref_logp[0]) - (seq_logp[1] - ref_logp[1]))
    dpo_loss = jax.nn.softplus(-margin)
    pull_scale = LOSS_SCALE * DPO_BETA * jax.nn.sigmoid(-margin)
    seq_coef = jnp.stack([-pull_scale, pull_scale])
    row_coef = jnp.sum(member * seq_coef[None, :], axis=1)
    softmax_rows = jnp.exp(logits - lse[:, None])
    grad_logits = (row_coef[:, None] * (matches.astype(jnp.float32) - softmax_rows)).astype(jnp.bfloat16)
    d_weight = lax.dot_general(hidden, grad_logits, (((0,), (0,)), ((), ())), preferred_element_type=jnp.float32).astype(jnp.bfloat16)
    d_hidden = lax.dot_general(grad_logits, weight, (((1,), (1,)), ((), ())), preferred_element_type=jnp.float32).astype(jnp.bfloat16)
    return (dpo_loss, d_hidden, d_weight)
```

```python
import functools

import jax
import jax.numpy as jnp
from jax import lax
from jax.experimental import pallas as pl
from jax.experimental.pallas import tpu as pltpu
from jax.sharding import PartitionSpec as P

MESH = pl.DeviceIdType.MESH
F32 = jnp.float32
BF16 = jnp.bfloat16

DPO_BETA = 0.01
LOSS_SCALE = 1024.0

NX, NY, NZ = 4, 4, 8
ROWS = 512
D = 8192
VSH = 384
HALF = 4096

GA, GB, GQ = 1024, 1536, 384
SX, SY, SZ = 384, 384, 256

N_SEM = 200


def fused_kernel(
    hid_ref, w_ref, tgt_ref, seq_ref, ref_ref,
    all_ref, grad_ref, loss_ref, dh_ref,
    H, W, logits_t, G,
    st_own, st_core, st_xy, st_z,
    psx, psy, psz, plx, ply, plz, sx, sy, sz,
    lx1, lx2, lx3, ly1, ly2, ly3, lz1h, lz1, lz2, lz3,
    rx2, ry2,
    local_sem, ssem, rsem,
):
    ctx = lax.axis_index("ctx")
    tp = lax.axis_index("tp")
    y = ctx // NZ
    z = lax.rem(ctx, NZ)
    x = tp // 2
    c = lax.rem(tp, 2)

    def wrap(v, n):
        return lax.rem(v + n, n)

    def dev(dy=0, dz=0, dx=0, dc=0):
        yy = wrap(y + dy, NY) if dy else y
        zz = wrap(z + dz, NZ) if dz else z
        xx = wrap(x + dx, NX) if dx else x
        cc = 1 - c if dc else c
        return (yy * NZ + zz, xx * 2 + cc)

    counter = [0]
    sends = []

    def remote(src, dst, **d):
        i = counter[0]
        counter[0] += 1
        copy = pltpu.make_async_remote_copy(
            src_ref=src, dst_ref=dst, send_sem=ssem.at[i], recv_sem=rsem.at[i],
            device_id=dev(**d), device_id_type=MESH,
        )
        copy.start()
        sends.append(copy)
        return copy

    def drain():
        for copy in sends:
            copy.wait_send()
        sends.clear()

    c0 = c * HALF
    col_a = pl.multiple_of(c0, 128)
    col_b = pl.multiple_of(c0 + GA, 128)
    col_q0 = pl.multiple_of(c0 + GA + GB, 128)
    col_q = pl.multiple_of(c0 + GA + GB + x * GQ, 128)

    w_load = pltpu.make_async_copy(w_ref, W, local_sem.at[0])
    w_load.start()
    own_ab = pltpu.make_async_copy(
        hid_ref.at[:, pl.ds(col_a, GA + GB)], H.at[y, z, :, pl.ds(col_a, GA + GB)], local_sem.at[1]
    )
    own_ab.start()
    own_q = pltpu.make_async_copy(
        hid_ref.at[:, pl.ds(col_q, GQ)], H.at[y, z, :, pl.ds(col_q, GQ)], local_sem.at[2]
    )
    own_q.start()

    barrier = pltpu.get_barrier_semaphore()
    peers = [dict(dc=1)]
    peers += [dict(dx=i, dy=j) for i in range(NX) for j in range(NY) if i or j]
    peers += [dict(dz=k) for k in range(1, NZ)]
    for p in peers:
        pl.semaphore_signal(barrier, inc=1, device_id=dev(**p), device_id_type=MESH)
    pl.semaphore_wait(barrier, len(peers))
    own_ab.wait()
    own_q.wait()

    def blk_a(zz):
        return H.at[:, zz, :, pl.ds(col_a, GA)]

    def blk_b(yy, zz):
        return H.at[yy, zz, :, pl.ds(col_b, GB)]

    def blk_q(zz):
        return H.at[:, zz, :, pl.ds(col_q, GQ)]

    own_a = H.at[y, z, :, pl.ds(col_a, GA)]
    own_qb = H.at[y, z, :, pl.ds(col_q, GQ)]
    first_a = [remote(own_a, own_a, dy=j) for j in (1, 2, 3)]
    first_q = [remote(own_qb, own_qb, dy=j) for j in (1, 2, 3)]

    def both_ways(ref):
        return (remote(ref, ref, dz=1), remote(ref, ref, dz=-1))

    def fan_y(zz):
        return [remote(blk_b(y, zz), blk_b(y, zz), dy=j) for j in (1, 2, 3)]

    def fan_x(zz):
        return [remote(blk_q(zz), blk_q(zz), dx=j) for j in (1, 2, 3)]

    def hand_over(ref):
        return remote(ref, ref, dc=1)

    handed = []
    waiting = []

    def hand_waiting():
        for zz, from_y, from_x in waiting:
            for copy in from_y:
                copy.wait_recv()
            handed.append(hand_over(H.at[:, zz, :, pl.ds(col_b, GB)]))
            for copy in from_x:
                copy.wait_recv()
            handed.append(hand_over(H.at[:, zz, :, pl.ds(col_q0, NX * GQ)]))
        waiting.clear()

    ring_b = both_ways(blk_b(y, z))
    fy = fan_y(z)
    for copy in first_a:
        copy.wait_recv()
    ring_a = both_ways(blk_a(z))
    for copy in first_q:
        copy.wait_recv()
    ring_q = both_ways(blk_q(z))
    fx = fan_x(z)
    handed.append(hand_over(blk_a(z)))
    waiting.append((z, fy, fx))

    def halves(yy, zz, col, n, k):
        cut = n // 256 * 128
        lo = col if k == 0 else pl.multiple_of(col + cut, 128)
        return H.at[yy, zz, :, pl.ds(lo, cut if k == 0 else n - cut)]

    for s in (1, 2, 3):
        now = []
        nb, na, nq = [], [], []
        for k, sign in ((0, 1), (1, -1)):
            zz = wrap(z - sign * s, NZ)
            ring_b[k].wait_recv()
            ref = blk_b(y, zz) if s < 3 else halves(y, zz, col_b, GB, k)
            nb.append(remote(ref, ref, dz=sign))
            fy = fan_y(zz)
            ring_q[k].wait_recv()
            ref = blk_q(zz) if s < 3 else halves(slice(None), zz, col_q, GQ, k)
            nq.append(remote(ref, ref, dz=sign))
            fx = fan_x(zz)
            ring_a[k].wait_recv()
            ref = blk_a(zz) if s < 3 else halves(slice(None), zz, col_a, GA, k)
            na.append(remote(ref, ref, dz=sign))
            handed.append(hand_over(blk_a(zz)))
            now.append((zz, fy, fx))
        hand_waiting()
        waiting.extend(now)
        ring_b, ring_a, ring_q = nb, na, nq

    zz = wrap(z + 4, NZ)
    ring_b[0].wait_recv()
    ring_b[1].wait_recv()
    fy = fan_y(zz)
    ring_q[0].wait_recv()
    ring_q[1].wait_recv()
    fx = fan_x(zz)
    ring_a[0].wait_recv()
    ring_a[1].wait_recv()
    handed.append(hand_over(blk_a(zz)))
    hand_waiting()
    waiting.append((zz, fy, fx))
    hand_waiting()
    for copy in handed:
        copy.wait_recv()
    drain()

    all_copy = pltpu.make_async_copy(H, all_ref, local_sem.at[1])
    all_copy.start()
    w_load.wait()

    KC = 1024
    acc = jnp.zeros((ROWS, VSH), F32)
    for k in range(D // KC):
        h = H[:, :, :, k * KC:(k + 1) * KC].reshape(ROWS, KC)
        acc = acc + jnp.dot(h, W[k * KC:(k + 1) * KC, :], preferred_element_type=F32)
    lt = acc.T
    logits_t[...] = lt

    def lanes(ref4):
        return jnp.concatenate([ref4[i:i + 1, :] for i in range(4)], axis=1)

    targets = lanes(tgt_ref[...])
    first_col = (ctx * 8 + tp) * VSH
    cols = first_col + lax.broadcasted_iota(jnp.int32, (VSH, ROWS), 0)
    matches = cols == targets
    peak = jnp.max(lt, axis=0, keepdims=True)
    local_lse = peak + jnp.log(jnp.sum(jnp.exp(lt - peak), axis=0, keepdims=True))
    picked = jnp.sum(jnp.where(matches, lt, 0.0), axis=0, keepdims=True)
    for i in range(4):
        st_own[0, i:i + 1, :] = local_lse[:, i * 128:(i + 1) * 128]
        st_own[0, 4 + i:5 + i, :] = picked[:, i * 128:(i + 1) * 128]

    def merge(mine, others):
        every = [mine] + others
        top = functools.reduce(jnp.maximum, every)
        total = functools.reduce(jnp.add, [jnp.exp(e - top) for e in every])
        summed = functools.reduce(jnp.add, every)
        row = lax.broadcasted_iota(jnp.int32, (8, 128), 0)
        return jnp.where(row < 4, top + jnp.log(total), summed)

    copy = remote(st_own.at[0], st_core, dc=1)
    copy.wait_recv()
    st = merge(st_own[0], [st_core[...]])
    st_own[1] = st
    group = [(i, j) for i in range(NX) for j in range(NY) if i or j]
    copies = [remote(st_own.at[1], st_xy.at[n], dx=i, dy=j) for n, (i, j) in enumerate(group)]
    for copy in copies:
        copy.wait_recv()
    st = merge(st, [st_xy[n] for n in range(15)])
    st_own[2] = st
    copies = [remote(st_own.at[2], st_z.at[k - 1], dz=k) for k in range(1, NZ)]
    for copy in copies:
        copy.wait_recv()
    st = merge(st, [st_z[n] for n in range(7)])
    lse4 = st[0:4, :]
    logp4 = st[4:8, :] - lse4
    seq4 = seq_ref[...]

    def total_of(v):
        return jnp.sum(jnp.sum(v, axis=1, keepdims=True), axis=0, keepdims=True)

    seq0 = total_of(jnp.where(seq4 == 0, logp4, 0.0))
    seq1 = total_of(jnp.where(seq4 == 1, logp4, 0.0))
    margin = DPO_BETA * ((seq0 - ref_ref[0]) - (seq1 - ref_ref[1]))
    neg = jnp.broadcast_to(-margin, (8, 128))
    loss_ref[...] = jnp.maximum(neg, 0.0) + jnp.log1p(jnp.exp(-jnp.abs(neg)))
    pull = (LOSS_SCALE * DPO_BETA) / (1.0 + jnp.exp(margin))
    coef4 = jnp.where(seq4 == 0, -pull, jnp.where(seq4 == 1, pull, 0.0))
    lse = lanes(lse4)
    coef = lanes(coef4)
    lt = logits_t[...]
    g_t = coef * (matches.astype(F32) - jnp.exp(lt - lse))
    g = g_t.T.astype(BF16)
    G[...] = g
    grad_copy = pltpu.make_async_copy(G, grad_ref, local_sem.at[2])
    grad_copy.start()

    def partial_of(xx, cc, off, n):
        start = pl.multiple_of((xx * 2 + cc) * 1024 + off, 128)
        return lax.dot_general(
            G[...], W[pl.ds(start, n), :], (((1,), (1,)), ((), ())), preferred_element_type=F32
        ).reshape(NY, NZ, 16, n)

    part_x = (psx, plx, sx, 0, SX)
    part_y = (psy, ply, sy, SX, SY)
    part_z = (psz, plz, sz, SX + SY, SZ)
    order = [(part_x, 2)] + [(part_z, j) for j in range(4)] + [(part_y, j) for j in range(4)]
    order += [(part_x, 1), (part_x, 3), (part_x, 0)]
    swaps = []
    for (ps, plnd, _, off, n), j in order:
        xx = wrap(x + j, NX)
        ps[xx] = partial_of(xx, 1 - c, off, n).astype(BF16)
        swaps.append(remote(ps.at[xx], plnd.at[xx], dc=1))

    def own_chunk(i):
        (_, plnd, s, off, n), j = order[i]
        xx = wrap(x + j, NX)
        mine = partial_of(xx, c, off, n)
        swaps[i].wait_recv()
        s[xx] = (mine + plnd[xx].astype(F32)).astype(BF16)

    def send_x(j):
        return remote(sx.at[wrap(x + j, NX)], lx1.at[j - 1], dx=j)

    def add(ref, idx, *others):
        total = ref[idx].astype(F32)
        for o in others:
            total = total + o.astype(F32)
        return total.astype(BF16)

    own_chunk(0)
    cx = {2: send_x(2)}
    for i in range(1, 5):
        own_chunk(i)
    zh = SZ // 2
    zr = remote(sz.at[:, :, wrap(z + 4, NZ), :, 0:zh], lz1h.at[0], dz=1)
    zl = remote(sz.at[:, :, wrap(z + 4, NZ), :, zh:SZ], lz1h.at[1], dz=-1)
    for i in range(5, 9):
        own_chunk(i)
    cy = [remote(sy.at[:, wrap(y + j, NY)], ly1.at[j - 1], dy=j) for j in (1, 2, 3)]

    def z_step(k, zr, zl):
        right, left = wrap(z + k, NZ), wrap(z - k, NZ)
        zr.wait_recv()
        zl.wait_recv()
        if k == 3:
            r_in, l_in = lz1h[0], lz1h[1]
            sz[:, :, right, :, 0:zh] = (sz[:, :, right, :, 0:zh].astype(F32) + r_in.astype(F32)).astype(BF16)
            sz[:, :, left, :, zh:SZ] = (sz[:, :, left, :, zh:SZ].astype(F32) + l_in.astype(F32)).astype(BF16)
        else:
            n = 2 - k
            sz[:, :, right] = (sz[:, :, right].astype(F32) + lz1[n, 0].astype(F32)).astype(BF16)
            sz[:, :, left] = (sz[:, :, left].astype(F32) + lz1[n, 1].astype(F32)).astype(BF16)
        n = 3 - k
        return (
            remote(sz.at[:, :, right], lz1.at[n, 0], dz=1),
            remote(sz.at[:, :, left], lz1.at[n, 1], dz=-1),
        )

    zr, zl = z_step(3, zr, zl)
    own_chunk(9)
    cx[1] = send_x(1)
    own_chunk(10)
    cx[3] = send_x(3)
    own_chunk(11)
    zr, zl = z_step(2, zr, zl)
    zr, zl = z_step(1, zr, zl)

    for j in (1, 2, 3):
        cx[j].wait_recv()
    for yy in range(NY):
        sx[x, yy] = add(sx, (x, yy), lx1[0, yy], lx1[1, yy], lx1[2, yy])
    cx = [remote(sx.at[x, wrap(y + j, NY)], lx2.at[j - 1], dy=j) for j in (1, 2, 3)]
    for copy in cy:
        copy.wait_recv()
    for xx in range(NX):
        sy[xx, y] = add(sy, (xx, y), ly1[0, xx], ly1[1, xx], ly1[2, xx])
    cy = [remote(sy.at[wrap(x + j, NX), y], ly2.at[j - 1], dx=j) for j in (1, 2, 3)]
    zr.wait_recv()
    zl.wait_recv()
    for xx in range(NX):
        sz[xx, :, z] = (
            sz[xx, :, z].astype(F32) + lz1[2, 0, xx].astype(F32) + lz1[2, 1, xx].astype(F32)
        ).astype(BF16)
    cz = [remote(sz.at[wrap(x + j, NX), :, z], lz2.at[j - 1], dx=j) for j in (1, 2, 3)]

    for copy in cx:
        copy.wait_recv()
    rx2[...] = add(sx, (x, y), lx2[0], lx2[1], lx2[2])
    cx = [remote(rx2.at[wrap(z + k, NZ)], lx3.at[k - 1], dz=k) for k in range(1, NZ)]
    for copy in cy:
        copy.wait_recv()
    ry2[...] = add(sy, (x, y), ly2[0], ly2[1], ly2[2])
    cy = [remote(ry2.at[wrap(z + k, NZ)], ly3.at[k - 1], dz=k) for k in range(1, NZ)]
    for copy in cz:
        copy.wait_recv()
    sz[x, :, z] = (
        sz[x, :, z].astype(F32) + lz2[0].astype(F32) + lz2[1].astype(F32) + lz2[2].astype(F32)
    ).astype(BF16)
    cz = [remote(sz.at[x, wrap(y + j, NY), z], lz3.at[j - 1], dy=j) for j in (1, 2, 3)]

    for copy in cx:
        copy.wait_recv()
    total = rx2[z].astype(F32)
    for k in range(7):
        total = total + lx3[k].astype(F32)
    dh_ref[:, 0:SX] = total.astype(BF16)
    for copy in cy:
        copy.wait_recv()
    total = ry2[z].astype(F32)
    for k in range(7):
        total = total + ly3[k].astype(F32)
    dh_ref[:, SX:SX + SY] = total.astype(BF16)
    for copy in cz:
        copy.wait_recv()
    total = sz[x, y, z].astype(F32)
    for k in range(3):
        total = total + lz3[k].astype(F32)
    dh_ref[:, SX + SY:] = total.astype(BF16)

    drain()
    all_copy.wait()
    grad_copy.wait()


def on_device(hidden, weight, targets, row_seq, ref_logp):
    vmem = pl.BlockSpec(memory_space=pltpu.VMEM)
    hbm = pl.BlockSpec(memory_space=pl.ANY)
    smem = pl.BlockSpec(memory_space=pltpu.SMEM)

    def v16(*shape):
        return pltpu.VMEM(shape, BF16)

    chunks = [v16(NX, NY, NZ, 16, n) for n in (SX, SY, SZ)]
    all_rows, grad, loss, d_hidden = pl.pallas_call(
        fused_kernel,
        out_shape=(
            jax.ShapeDtypeStruct((NY, NZ, 16, D), BF16),
            jax.ShapeDtypeStruct((ROWS, VSH), BF16),
            jax.ShapeDtypeStruct((8, 128), F32),
            jax.ShapeDtypeStruct((16, 1024), BF16),
        ),
        in_specs=[hbm, hbm, vmem, vmem, smem],
        out_specs=(hbm, hbm, vmem, vmem),
        scratch_shapes=[
            v16(NY, NZ, 16, D),
            v16(D, VSH),
            pltpu.VMEM((VSH, ROWS), F32),
            v16(ROWS, VSH),
            pltpu.VMEM((3, 8, 128), F32),
            pltpu.VMEM((8, 128), F32),
            pltpu.VMEM((15, 8, 128), F32),
            pltpu.VMEM((7, 8, 128), F32),
            *chunks, *chunks, *chunks,
            v16(3, NY, NZ, 16, SX), v16(3, NZ, 16, SX), v16(7, 16, SX),
            v16(3, NX, NZ, 16, SY), v16(3, NZ, 16, SY), v16(7, 16, SY),
            v16(2, NX, NY, 16, SZ // 2), v16(3, 2, NX, NY, 16, SZ), v16(3, NY, 16, SZ), v16(3, 16, SZ),
            v16(NZ, 16, SX), v16(NZ, 16, SY),
            pltpu.SemaphoreType.DMA((3,)),
            pltpu.SemaphoreType.DMA((N_SEM,)),
            pltpu.SemaphoreType.DMA((N_SEM,)),
        ],
        compiler_params=pltpu.CompilerParams(
            collective_id=0, has_side_effects=True, vmem_limit_bytes=56 * 2**20
        ),
        cost_estimate=pl.CostEstimate(flops=2 * 2 * ROWS * D * VSH, bytes_accessed=2 * D * VSH, transcendentals=0),
    )(hidden, weight, targets.reshape(4, 128), row_seq.reshape(4, 128), ref_logp)
    d_weight = lax.dot_general(
        all_rows.reshape(ROWS, D), grad, (((0,), (0,)), ((), ())), preferred_element_type=F32
    ).astype(BF16)
    return (loss[0, 0], d_hidden, d_weight)


def solution(mesh):
    placed = (P("ctx", None), P(None, ("ctx", "tp")), P(), P(), P())
    return jax.shard_map(
        on_device,
        mesh=mesh,
        in_specs=placed,
        out_specs=(P(), P("ctx", "tp"), P(None, ("ctx", "tp"))),
        check_vma=False,
    )
```

```python
import functools

import jax
import jax.numpy as jnp
from jax import lax
from jax.experimental import pallas as pl
from jax.experimental.pallas import tpu as pltpu
from jax.sharding import PartitionSpec as P

MESH = pl.DeviceIdType.MESH
F32 = jnp.float32
BF16 = jnp.bfloat16

DPO_BETA = 0.01
LOSS_SCALE = 1024.0

NX, NY, NZ = 4, 4, 8
ROWS = 512
D = 8192
VSH = 384
HALF = 4096

GA, GB, GQ = 1024, 1536, 384
SX, SY, SZ = 384, 384, 256

N_SEM = 200

KC = 1024


def fused_kernel(
    hid_ref, w_ref, tgt_ref, seq_ref, ref_ref,
    dw_ref, loss_ref, dh_ref,
    H, W, L, logits_t, G,
    st_own, st_core, st_xy, st_z,
    psx, psy, psz, plx, ply, plz, sx, sy, sz,
    hx, lx1, lx2, lx3, hy, ly1, ly2, ly3, lz3s, lz4s, lz1, lz2, lz5, lz3,
    local_sem, ssem, rsem,
):
    ctx = lax.axis_index("ctx")
    tp = lax.axis_index("tp")
    y = ctx // NZ
    z = lax.rem(ctx, NZ)
    x = tp // 2
    c = lax.rem(tp, 2)

    def wrap(v, n):
        return lax.rem(v + n, n)

    def dev(dy=0, dz=0, dx=0, dc=0):
        yy = wrap(y + dy, NY) if dy else y
        zz = wrap(z + dz, NZ) if dz else z
        xx = wrap(x + dx, NX) if dx else x
        cc = 1 - c if dc else c
        return (yy * NZ + zz, xx * 2 + cc)

    counter = [0]
    sends = []

    def remote(src, dst, **d):
        i = counter[0]
        counter[0] += 1
        copy = pltpu.make_async_remote_copy(
            src_ref=src, dst_ref=dst, send_sem=ssem.at[i], recv_sem=rsem.at[i],
            device_id=dev(**d), device_id_type=MESH,
        )
        copy.start()
        sends.append(copy)
        return copy

    def rx(copy):
        copy.wait_recv()

    def drain():
        for copy in sends:
            copy.wait_send()
        sends.clear()

    c0 = c * HALF
    col_a = pl.multiple_of(c0, 128)
    col_b = pl.multiple_of(c0 + GA, 128)
    col_q0 = pl.multiple_of(c0 + GA + GB, 128)
    col_q = pl.multiple_of(c0 + GA + GB + x * GQ, 128)

    w_load = pltpu.make_async_copy(w_ref, W, local_sem.at[0])
    w_load.start()
    own_ab = pltpu.make_async_copy(
        hid_ref.at[:, pl.ds(col_a, GA + GB)], H.at[y, z, :, pl.ds(col_a, GA + GB)], local_sem.at[1]
    )
    own_ab.start()
    own_q = pltpu.make_async_copy(
        hid_ref.at[:, pl.ds(col_q, GQ)], H.at[y, z, :, pl.ds(col_q, GQ)], local_sem.at[2]
    )
    own_q.start()

    barrier = pltpu.get_barrier_semaphore()
    peers = [dict(dc=1)]
    peers += [dict(dx=i, dy=j) for i in range(NX) for j in range(NY) if i or j]
    peers += [dict(dz=k) for k in range(1, NZ)]
    for p in peers:
        pl.semaphore_signal(barrier, inc=1, device_id=dev(**p), device_id_type=MESH)
    pl.semaphore_wait(barrier, len(peers))
    own_ab.wait()
    own_q.wait()

    def blk_a(zz):
        return H.at[:, zz, :, pl.ds(col_a, GA)]

    def blk_b(yy, zz):
        return H.at[yy, zz, :, pl.ds(col_b, GB)]

    def blk_q(zz):
        return H.at[:, zz, :, pl.ds(col_q, GQ)]

    own_a = H.at[y, z, :, pl.ds(col_a, GA)]
    own_qb = H.at[y, z, :, pl.ds(col_q, GQ)]
    first_a = [remote(own_a, own_a, dy=j) for j in (1, 2, 3)]
    first_q = [remote(own_qb, own_qb, dy=j) for j in (1, 2, 3)]

    def both_ways(ref):
        return (remote(ref, ref, dz=1), remote(ref, ref, dz=-1))

    def fan_y(zz):
        return [remote(blk_b(y, zz), blk_b(y, zz), dy=j) for j in (1, 2, 3)]

    def fan_x(zz):
        return [remote(blk_q(zz), blk_q(zz), dx=j) for j in (1, 2, 3)]

    def hand_over(ref):
        return remote(ref, ref, dc=1)

    handed = {}
    arrivals = {}

    def hand_on(key, zz):
        from_y, from_x = arrivals.pop(key)
        for copy in from_y:
            rx(copy)
        handed[key].append(hand_over(H.at[:, zz, :, pl.ds(col_b, GB)]))
        for copy in from_x:
            rx(copy)
        handed[key].append(hand_over(H.at[:, zz, :, pl.ds(col_q0, NX * GQ)]))

    def logits_of(keys):
        zs = [wrap(z - sign * st, NZ) for st, sign in keys]
        for key in keys:
            for copy in handed[key]:
                rx(copy)
        def step(k, acc):
            at = pl.ds(pl.multiple_of(k * KC, KC), KC)
            h = jnp.concatenate([H[yy, zz, :, at] for zz in zs for yy in range(NY)], axis=0)
            return acc + jnp.dot(h, W[at, :], preferred_element_type=F32)

        acc = lax.fori_loop(0, D // KC, step, jnp.zeros((64 * len(zs), VSH), F32))
        acc = acc.reshape(len(zs), NY, 16, VSH)
        for n, zz in enumerate(zs):
            L[:, zz] = acc[n]

    ring_b = both_ways(blk_b(y, z))
    fy = fan_y(z)
    for copy in first_a:
        rx(copy)
    ring_a = both_ways(blk_a(z))
    for copy in first_q:
        rx(copy)
    ring_q = both_ways(blk_q(z))
    fx = fan_x(z)
    handed[0, 1] = [hand_over(blk_a(z))]
    arrivals[0, 1] = (fy, fx)

    def halves(yy, zz, col, n, k):
        cut = n // 256 * 128
        lo = col if k == 0 else pl.multiple_of(col + cut, 128)
        return H.at[yy, zz, :, pl.ds(lo, cut if k == 0 else n - cut)]

    for s in (1, 2, 3):
        nb, na, nq = [], [], []
        for k, sign in ((0, 1), (1, -1)):
            zz = wrap(z - sign * s, NZ)
            rx(ring_b[k])
            ref = blk_b(y, zz) if s < 3 else halves(y, zz, col_b, GB, k)
            nb.append(remote(ref, ref, dz=sign))
            fy = fan_y(zz)
            rx(ring_q[k])
            ref = blk_q(zz) if s < 3 else halves(slice(None), zz, col_q, GQ, k)
            nq.append(remote(ref, ref, dz=sign))
            fx = fan_x(zz)
            rx(ring_a[k])
            ref = blk_a(zz) if s < 3 else halves(slice(None), zz, col_a, GA, k)
            na.append(remote(ref, ref, dz=sign))
            handed[s, sign] = [hand_over(blk_a(zz))]
            arrivals[s, sign] = (fy, fx)
        for key in list(arrivals):
            if key[0] < s:
                hand_on(key, wrap(z - key[1] * key[0], NZ))
        if s == 2:
            w_load.wait()
        if s == 3:
            logits_of([(1, 1), (1, -1)])
        ring_b, ring_a, ring_q = nb, na, nq

    zz = wrap(z + 4, NZ)
    rx(ring_b[0])
    rx(ring_b[1])
    fy = fan_y(zz)
    rx(ring_q[0])
    rx(ring_q[1])
    fx = fan_x(zz)
    rx(ring_a[0])
    rx(ring_a[1])
    handed[4, -1] = [hand_over(blk_a(zz))]
    arrivals[4, -1] = (fy, fx)
    hand_on((3, 1), wrap(z - 3, NZ))
    hand_on((3, -1), wrap(z + 3, NZ))
    logits_of([(2, 1), (2, -1)])
    hand_on((4, -1), zz)
    logits_of([(3, 1), (3, -1)])
    logits_of([(0, 1), (4, -1)])
    drain()

    lt = L[...].reshape(ROWS, VSH).T
    logits_t[...] = lt

    def lanes(ref4):
        return jnp.concatenate([ref4[i:i + 1, :] for i in range(4)], axis=1)

    targets = lanes(tgt_ref[...])
    first_col = (ctx * 8 + tp) * VSH
    cols = first_col + lax.broadcasted_iota(jnp.int32, (VSH, ROWS), 0)
    matches = cols == targets
    peak = jnp.max(lt, axis=0, keepdims=True)
    local_lse = peak + jnp.log(jnp.sum(jnp.exp(lt - peak), axis=0, keepdims=True))
    picked = jnp.sum(jnp.where(matches, lt, 0.0), axis=0, keepdims=True)
    for i in range(4):
        st_own[0, i:i + 1, :] = local_lse[:, i * 128:(i + 1) * 128]
        st_own[0, 4 + i:5 + i, :] = picked[:, i * 128:(i + 1) * 128]

    def merge(mine, others):
        every = [mine] + others
        top = functools.reduce(jnp.maximum, every)
        total = functools.reduce(jnp.add, [jnp.exp(e - top) for e in every])
        summed = functools.reduce(jnp.add, every)
        row = lax.broadcasted_iota(jnp.int32, (8, 128), 0)
        return jnp.where(row < 4, top + jnp.log(total), summed)

    copy = remote(st_own.at[0], st_core, dc=1)
    rx(copy)
    st = merge(st_own[0], [st_core[...]])
    st_own[1] = st
    group = [(i, j) for i in range(NX) for j in range(NY) if i or j]
    copies = [remote(st_own.at[1], st_xy.at[n], dx=i, dy=j) for n, (i, j) in enumerate(group)]
    for copy in copies:
        rx(copy)
    st = merge(st, [st_xy[n] for n in range(15)])
    st_own[2] = st
    copies = [remote(st_own.at[2], st_z.at[k - 1], dz=k) for k in range(1, NZ)]
    for copy in copies:
        rx(copy)
    st = merge(st, [st_z[n] for n in range(7)])
    lse4 = st[0:4, :]
    logp4 = st[4:8, :] - lse4
    seq4 = seq_ref[...]

    def total_of(v):
        return jnp.sum(jnp.sum(v, axis=1, keepdims=True), axis=0, keepdims=True)

    seq0 = total_of(jnp.where(seq4 == 0, logp4, 0.0))
    seq1 = total_of(jnp.where(seq4 == 1, logp4, 0.0))
    margin = DPO_BETA * ((seq0 - ref_ref[0]) - (seq1 - ref_ref[1]))
    neg = jnp.broadcast_to(-margin, (8, 128))
    loss_ref[...] = jnp.maximum(neg, 0.0) + jnp.log1p(jnp.exp(-jnp.abs(neg)))
    pull = (LOSS_SCALE * DPO_BETA) / (1.0 + jnp.exp(margin))
    coef4 = jnp.where(seq4 == 0, -pull, jnp.where(seq4 == 1, pull, 0.0))
    lse = lanes(lse4)
    coef = lanes(coef4)
    lt = logits_t[...]
    g_t = coef * (matches.astype(F32) - jnp.exp(lt - lse))
    g = g_t.T.astype(BF16)
    G[...] = g

    def weight_grad(first, last):
        n = 512

        def step(i, carry):
            at = pl.ds(pl.multiple_of(i * n, n), n)
            h = H[:, :, :, at].reshape(ROWS, n)
            dw_ref[at, :] = lax.dot_general(
                h, G[...], (((0,), (0,)), ((), ())), preferred_element_type=F32
            ).astype(BF16)
            return carry

        lax.fori_loop(first, last, step, 0)

    def product(rows, xx, cc, off, n):
        start = pl.multiple_of((xx * 2 + cc) * 1024 + off, 128)
        return lax.dot_general(
            rows, W[pl.ds(start, n), :], (((1,), (1,)), ((), ())), preferred_element_type=F32
        )

    def x_dot(j, cc):
        return [product(G[...], wrap(x + j, NX), cc, 0, SX).reshape(NY, NZ, 16, SX)]

    def y_dot(j, cc):
        rows = G[pl.ds(pl.multiple_of(wrap(y + j, NY) * 128, 128), 128), :]
        return [product(rows, xx, cc, SX, SY).reshape(NZ, 16, SY) for xx in range(NX)]

    def z_dot(j, cc):
        p = product(G[...], j, cc, SX + SY, SZ).reshape(NY, NZ, 16, SZ)
        return [p[:, zz] for zz in range(NZ)]

    def places(part, j):
        if part == "x":
            return [(wrap(x + j, NX),)], (wrap(x + j, NX),)
        if part == "y":
            return [(wrap(y + j, NY), xx) for xx in range(NX)], (wrap(y + j, NY),)
        return [(zz, j) for zz in range(NZ)], (slice(None), j)

    parts = {"x": (x_dot, psx, plx, sx), "y": (y_dot, psy, ply, sy), "z": (z_dot, psz, plz, sz)}
    swaps = {}

    def give(part, j):
        dot, ps, land, _ = parts[part]
        idx, whole = places(part, j)
        for at, p in zip(idx, dot(j, 1 - c)):
            ps[at] = p.astype(BF16)
        swaps[part, j] = remote(ps.at[whole], land.at[whole], dc=1)

    def keep(part, j, extra=None):
        dot, _, land, s = parts[part]
        idx, _ = places(part, j)
        mine = dot(j, c)
        rx(swaps[part, j])
        for at, p in zip(idx, mine):
            s[at] = (p + land[at].astype(F32)).astype(BF16)

    def bump(ref, at, *others):
        total = ref[at].astype(F32)
        for o in others:
            total = total + o.astype(F32)
        ref[at] = total.astype(BF16)

    lo, hi = slice(0, 2), slice(2, 4)

    def send_halves(s, h, me, n, **d):
        (axis,) = d
        far = wrap(me + 2, n)
        return (
            remote(s.at[far, lo], h.at[0], **{axis: 1}),
            remote(s.at[far, hi], h.at[1], **{axis: -1}),
        )

    def send_near(s, h, land, me, n, halves_in, side, axis):
        at = wrap(me + side, n)
        k = 0 if side == 1 else 1
        rx(halves_in[k])
        for i in (0, 1):
            bump(s, (at, 2 * k + i), h[k, i])
        return remote(s.at[at], land.at[k], **{axis: side})

    give("x", 2)
    give("y", 2)
    for j in range(4):
        give("z", j)
    keep("x", 2)
    xh = send_halves(sx, hx, x, NX, dx=0)
    keep("y", 2)
    yh = send_halves(sy, hy, y, NY, dy=0)
    give("x", 1)
    give("x", 3)
    for j in range(4):
        keep("z", j)

    def zat(k):
        return wrap(z + k, NZ)

    z3r = remote(sz.at[zat(3)], lz3s.at[0], dz=1)
    z3l = remote(sz.at[zat(-3)], lz3s.at[1], dz=-1)
    z4l = remote(sz.at[zat(4), lo], lz4s.at[0], dz=-2)
    z4r = remote(sz.at[zat(4), hi], lz4s.at[1], dz=2)
    z1r = remote(sz.at[zat(1)], lz1.at[0], dz=1)
    z1l = remote(sz.at[zat(-1)], lz1.at[1], dz=-1)
    give("y", 1)
    give("y", 3)
    give("x", 0)
    give("y", 0)
    weight_grad(0, 2)
    keep("x", 1)
    xr = send_near(sx, hx, lx1, x, NX, xh, 1, "dx")
    keep("x", 3)
    xl = send_near(sx, hx, lx1, x, NX, xh, -1, "dx")
    keep("y", 1)
    yr = send_near(sy, hy, ly1, y, NY, yh, 1, "dy")
    keep("y", 3)
    yl = send_near(sy, hy, ly1, y, NY, yh, -1, "dy")
    keep("x", 0)
    keep("y", 0)
    rx(z3r)
    rx(z3l)
    rx(z4l)
    rx(z4r)
    for i in range(NX):
        bump(sz, (zat(-2), i), lz3s[1, i], *([lz4s[0, i]] if i < 2 else []))
    z2l = remote(sz.at[zat(-2)], lz2.at[0], dz=-2)
    for i in range(NX):
        bump(sz, (zat(2), i), lz3s[0, i], *([lz4s[1, i - 2]] if i >= 2 else []))
    z2r = remote(sz.at[zat(2)], lz2.at[1], dz=2)
    weight_grad(2, 10)

    rx(xr)
    rx(xl)
    for yy in range(NY):
        bump(sx, (x, yy), lx1[0, yy], lx1[1, yy])
    cx = [remote(sx.at[x, wrap(y + j, NY)], lx2.at[j - 1], dy=j) for j in (1, 2, 3)]
    rx(yr)
    rx(yl)
    for xx in range(NX):
        bump(sy, (y, xx), ly1[0, xx], ly1[1, xx])
    cy = [remote(sy.at[y, wrap(x + j, NX)], ly2.at[j - 1], dx=j) for j in (1, 2, 3)]
    weight_grad(10, 12)
    for copy in (z1r, z1l, z2l, z2r):
        rx(copy)
    for xx in range(NX):
        bump(sz, (z, xx), lz1[0, xx], lz1[1, xx], lz2[0, xx], lz2[1, xx])
    cz = [remote(sz.at[z, wrap(x + j, NX)], lz5.at[j - 1], dx=j) for j in (1, 2, 3)]

    for copy in cx:
        rx(copy)
    bump(sx, (x, y), lx2[0], lx2[1], lx2[2])
    cx = [remote(sx.at[x, y, zat(k)], lx3.at[k - 1], dz=k) for k in range(1, NZ)]
    for copy in cy:
        rx(copy)
    bump(sy, (y, x), ly2[0], ly2[1], ly2[2])
    cy = [remote(sy.at[y, x, zat(k)], ly3.at[k - 1], dz=k) for k in range(1, NZ)]
    for copy in cz:
        rx(copy)
    bump(sz, (z, x), lz5[0], lz5[1], lz5[2])
    cz = [remote(sz.at[z, x, wrap(y + j, NY)], lz3.at[j - 1], dy=j) for j in (1, 2, 3)]
    weight_grad(12, 16)
    for copy in cx:
        rx(copy)
    total = sx[x, y, z].astype(F32)
    for k in range(7):
        total = total + lx3[k].astype(F32)
    dh_ref[:, 0:SX] = total.astype(BF16)
    for copy in cy:
        rx(copy)
    total = sy[y, x, z].astype(F32)
    for k in range(7):
        total = total + ly3[k].astype(F32)
    dh_ref[:, SX:SX + SY] = total.astype(BF16)
    for copy in cz:
        rx(copy)
    total = sz[z, x, y].astype(F32)
    for k in range(3):
        total = total + lz3[k].astype(F32)
    dh_ref[:, SX + SY:] = total.astype(BF16)

    drain()


def run_kernel(hidden, weight, targets, row_seq, ref_logp):
    vmem = pl.BlockSpec(memory_space=pltpu.VMEM)
    hbm = pl.BlockSpec(memory_space=pl.ANY)
    smem = pl.BlockSpec(memory_space=pltpu.SMEM)

    def v16(*shape):
        return pltpu.VMEM(shape, BF16)

    chunks = [v16(NX, NY, NZ, 16, SX), v16(NY, NX, NZ, 16, SY), v16(NZ, NX, NY, 16, SZ)]
    return pl.pallas_call(
        fused_kernel,
        out_shape=(
            pltpu.VMEM((D, VSH), BF16),
            pltpu.VMEM((8, 128), F32),
            pltpu.VMEM((16, 1024), BF16),
        ),
        in_specs=[hbm, hbm, vmem, vmem, smem],
        out_specs=(vmem, vmem, vmem),
        scratch_shapes=[
            v16(NY, NZ, 16, D),
            v16(D, VSH),
            pltpu.VMEM((NY, NZ, 16, VSH), F32),
            pltpu.VMEM((VSH, ROWS), F32),
            v16(ROWS, VSH),
            pltpu.VMEM((3, 8, 128), F32),
            pltpu.VMEM((8, 128), F32),
            pltpu.VMEM((15, 8, 128), F32),
            pltpu.VMEM((7, 8, 128), F32),
            *chunks, *chunks, *chunks,
            v16(2, 2, NZ, 16, SX), v16(2, NY, NZ, 16, SX), v16(3, NZ, 16, SX), v16(7, 16, SX),
            v16(2, 2, NZ, 16, SY), v16(2, NX, NZ, 16, SY), v16(3, NZ, 16, SY), v16(7, 16, SY),
            v16(2, NX, NY, 16, SZ), v16(2, 2, NY, 16, SZ), v16(2, NX, NY, 16, SZ),
            v16(2, NX, NY, 16, SZ), v16(3, NY, 16, SZ), v16(3, 16, SZ),
            pltpu.SemaphoreType.DMA((3,)),
            pltpu.SemaphoreType.DMA((N_SEM,)),
            pltpu.SemaphoreType.DMA((N_SEM,)),
        ],
        compiler_params=pltpu.CompilerParams(
            collective_id=0, has_side_effects=True, vmem_limit_bytes=52 * 2**20
        ),
        cost_estimate=pl.CostEstimate(flops=2 * 2 * ROWS * D * VSH, bytes_accessed=2 * D * VSH, transcendentals=0),
    )(hidden, weight, targets.reshape(4, 128), row_seq.reshape(4, 128), ref_logp)


def on_device(hidden, weight, targets, row_seq, ref_logp):
    dw, loss, dh = run_kernel(hidden, weight, targets, row_seq, ref_logp)

    def leave(dw_ref, loss_ref, dh_ref, dw_out, loss_out, dh_out, sem):
        copy = pltpu.make_async_copy(dw_ref, dw_out, sem.at[0])
        copy.start()
        loss_out[0] = loss_ref[0, 0]
        dh_out[...] = dh_ref[...]
        copy.wait()

    vmem = pl.BlockSpec(memory_space=pltpu.VMEM)
    d_weight, dpo_loss, d_hidden = pl.pallas_call(
        leave,
        out_shape=(
            jax.ShapeDtypeStruct((D, VSH), BF16),
            jax.ShapeDtypeStruct((1,), F32),
            jax.ShapeDtypeStruct((16, 1024), BF16),
        ),
        in_specs=[vmem, vmem, vmem],
        out_specs=(pl.BlockSpec(memory_space=pl.ANY), pl.BlockSpec(memory_space=pltpu.SMEM), vmem),
        scratch_shapes=[pltpu.SemaphoreType.DMA((1,))],
        compiler_params=pltpu.CompilerParams(has_side_effects=True, vmem_limit_bytes=16 * 2**20),
    )(dw, loss, dh)
    return (dpo_loss[0], d_hidden, d_weight)


def solution(mesh):
    placed = (P("ctx", None), P(None, ("ctx", "tp")), P(), P(), P())
    return jax.shard_map(
        on_device,
        mesh=mesh,
        in_specs=placed,
        out_specs=(P(), P("ctx", "tp"), P(None, ("ctx", "tp"))),
        check_vma=False,
    )
```

```python
import functools

import jax
import jax.numpy as jnp
from jax import lax
from jax.experimental import pallas as pl
from jax.experimental.pallas import tpu as pltpu
from jax.sharding import PartitionSpec as P

MESH = pl.DeviceIdType.MESH
F32 = jnp.float32
BF16 = jnp.bfloat16

DPO_BETA = 0.01
LOSS_SCALE = 1024.0

NX, NY, NZ = 4, 4, 8
ROWS = 512
D = 8192
VSH = 384
HALF = 4096

GA, GB, GQ = 1024, 1536, 384
SX, SY, SZ = 384, 384, 256

N_SEM = 53

KC = 1024


def fused_kernel(
    hid_ref, w_ref, tgt_ref, seq_ref, ref_ref,
    dw_ref, loss_ref, dh_ref,
    H, W, L, logits_t, G,
    st_own, st_core, st_xy, st_z,
    psx, psy, psz, plx, ply, plz, sx, sy, sz,
    hx, lx1, lx2, lx3, hy, ly1, ly2, ly3, lz3s, lz4s, lz1, lz2, lz5, lz3,
    local_sem, ssem, rsem,
):
    ctx = lax.axis_index("ctx")
    tp = lax.axis_index("tp")
    y = ctx // NZ
    z = lax.rem(ctx, NZ)
    x = tp // 2
    c = lax.rem(tp, 2)

    def wrap(v, n):
        return lax.rem(v + n, n)

    def dev(dy=0, dz=0, dx=0, dc=0):
        yy = wrap(y + dy, NY) if dy else y
        zz = wrap(z + dz, NZ) if dz else z
        xx = wrap(x + dx, NX) if dx else x
        cc = 1 - c if dc else c
        return (yy * NZ + zz, xx * 2 + cc)

    counter = [0]
    sends = []

    def number():
        counter[0] += 1
        return counter[0] - 1

    def remote(src, dst, i=None, **d):
        i_own = number() if i is None else i
        copy = pltpu.make_async_remote_copy(
            src_ref=src, dst_ref=dst, send_sem=ssem.at[i_own], recv_sem=rsem.at[i_own],
            device_id=dev(**d), device_id_type=MESH,
        )
        copy.start()
        if i is None:
            sends.append(copy)
            return copy

    def all_of(i, whole, **d):
        copy = pltpu.make_async_remote_copy(
            src_ref=whole, dst_ref=whole, send_sem=ssem.at[i], recv_sem=rsem.at[i],
            device_id=dev(**d), device_id_type=MESH,
        )
        sends.append(copy)
        return copy

    def fan(pairs, whole):
        i = number()
        for src, dst, d in pairs:
            remote(src, dst, i, **d)
        return all_of(i, whole, **pairs[0][2])

    def rx(copy):
        copy.wait_recv()

    def drain():
        for copy in sends:
            copy.wait_send()
        sends.clear()

    c0 = c * HALF
    col_a = pl.multiple_of(c0, 128)
    col_b = pl.multiple_of(c0 + GA, 128)
    col_q0 = pl.multiple_of(c0 + GA + GB, 128)
    col_q = pl.multiple_of(c0 + GA + GB + x * GQ, 128)

    w_load = pltpu.make_async_copy(w_ref, W, local_sem.at[0])
    w_load.start()
    own_ab = pltpu.make_async_copy(
        hid_ref.at[:, pl.ds(col_a, GA + GB)], H.at[y, z, :, pl.ds(col_a, GA + GB)], local_sem.at[1]
    )
    own_ab.start()
    own_q = pltpu.make_async_copy(
        hid_ref.at[:, pl.ds(col_q, GQ)], H.at[y, z, :, pl.ds(col_q, GQ)], local_sem.at[2]
    )
    own_q.start()

    barrier = pltpu.get_barrier_semaphore()
    peers = [dict(dc=1)]
    peers += [dict(dx=i, dy=j) for i in range(NX) for j in range(NY) if i or j]
    peers += [dict(dz=k) for k in range(1, NZ)]
    for p in peers:
        pl.semaphore_signal(barrier, inc=1, device_id=dev(**p), device_id_type=MESH)
    pl.semaphore_wait(barrier, len(peers))
    own_ab.wait()
    own_q.wait()

    def blk_a(zz):
        return H.at[:, zz, :, pl.ds(col_a, GA)]

    def blk_b(yy, zz):
        return H.at[yy, zz, :, pl.ds(col_b, GB)]

    def blk_q(zz):
        return H.at[:, zz, :, pl.ds(col_q, GQ)]

    own_a = H.at[y, z, :, pl.ds(col_a, GA)]
    own_qb = H.at[y, z, :, pl.ds(col_q, GQ)]
    first_a = fan([(own_a, own_a, dict(dy=j)) for j in (1, 2, 3)], H.at[0:3, z, :, pl.ds(col_a, GA)])
    first_q = fan([(own_qb, own_qb, dict(dy=j)) for j in (1, 2, 3)], H.at[0:3, z, :, pl.ds(col_q, GQ)])

    def both_ways(ref):
        return (remote(ref, ref, dz=1), remote(ref, ref, dz=-1))

    def fan_y(zz):
        ref = blk_b(y, zz)
        return fan([(ref, ref, dict(dy=j)) for j in (1, 2, 3)], H.at[0:3, zz, :, pl.ds(col_b, GB)])

    def fan_x(zz):
        ref = blk_q(zz)
        return fan([(ref, ref, dict(dx=j)) for j in (1, 2, 3)], H.at[:, zz, :, pl.ds(col_q0, 3 * GQ)])

    handed = {}
    arrivals = {}

    def hand_over(key, ref):
        if key not in handed:
            handed[key] = number()
        remote(ref, ref, handed[key], dc=1)

    def hand_on(key, zz):
        from_y, from_x = arrivals.pop(key)
        rx(from_y)
        hand_over(key, H.at[:, zz, :, pl.ds(col_b, GB)])
        rx(from_x)
        hand_over(key, H.at[:, zz, :, pl.ds(col_q0, NX * GQ)])
        handed[key] = all_of(handed[key], H.at[:, zz, :, pl.ds(col_a, HALF)], dc=1)

    def logits_of(keys):
        zs = [wrap(z - sign * st, NZ) for st, sign in keys]
        for key in keys:
            rx(handed[key])
        acc = jnp.zeros((64 * len(zs), VSH), F32)
        for k in range(0, D, KC):
            h = jnp.concatenate([H[yy, zz, :, k:k + KC] for zz in zs for yy in range(NY)], axis=0)
            acc = acc + jnp.dot(h, W[k:k + KC, :], preferred_element_type=F32)
        acc = acc.reshape(len(zs), NY, 16, VSH)
        for n, zz in enumerate(zs):
            L[:, zz] = acc[n]

    ring_b = both_ways(blk_b(y, z))
    fy = fan_y(z)
    rx(first_a)
    ring_a = both_ways(blk_a(z))
    rx(first_q)
    ring_q = both_ways(blk_q(z))
    fx = fan_x(z)
    hand_over((0, 1), blk_a(z))
    arrivals[0, 1] = (fy, fx)

    def halves(yy, zz, col, n, k):
        cut = n // 256 * 128
        lo = col if k == 0 else pl.multiple_of(col + cut, 128)
        return H.at[yy, zz, :, pl.ds(lo, cut if k == 0 else n - cut)]

    for s in (1, 2, 3):
        nb, na, nq = [], [], []
        for k, sign in ((0, 1), (1, -1)):
            zz = wrap(z - sign * s, NZ)
            rx(ring_b[k])
            ref = blk_b(y, zz) if s < 3 else halves(y, zz, col_b, GB, k)
            nb.append(remote(ref, ref, dz=sign))
            fy = fan_y(zz)
            rx(ring_q[k])
            ref = blk_q(zz) if s < 3 else halves(slice(None), zz, col_q, GQ, k)
            nq.append(remote(ref, ref, dz=sign))
            fx = fan_x(zz)
            rx(ring_a[k])
            ref = blk_a(zz) if s < 3 else halves(slice(None), zz, col_a, GA, k)
            na.append(remote(ref, ref, dz=sign))
            hand_over((s, sign), blk_a(zz))
            arrivals[s, sign] = (fy, fx)
        for key in list(arrivals):
            if key[0] < s:
                hand_on(key, wrap(z - key[1] * key[0], NZ))
        if s == 2:
            w_load.wait()
        if s == 3:
            logits_of([(1, 1), (1, -1)])
        ring_b, ring_a, ring_q = nb, na, nq

    zz = wrap(z + 4, NZ)
    rx(ring_b[0])
    rx(ring_b[1])
    fy = fan_y(zz)
    rx(ring_q[0])
    rx(ring_q[1])
    fx = fan_x(zz)
    rx(ring_a[0])
    rx(ring_a[1])
    hand_over((4, -1), blk_a(zz))
    arrivals[4, -1] = (fy, fx)
    hand_on((3, 1), wrap(z - 3, NZ))
    hand_on((3, -1), wrap(z + 3, NZ))
    logits_of([(2, 1), (2, -1)])
    hand_on((4, -1), zz)
    logits_of([(3, 1), (3, -1)])
    logits_of([(0, 1), (4, -1)])
    drain()

    lt = L[...].reshape(ROWS, VSH).T
    logits_t[...] = lt

    def lanes(ref4):
        return jnp.concatenate([ref4[i:i + 1, :] for i in range(4)], axis=1)

    targets = lanes(tgt_ref[...])
    first_col = (ctx * 8 + tp) * VSH
    cols = first_col + lax.broadcasted_iota(jnp.int32, (VSH, ROWS), 0)
    matches = cols == targets
    peak = jnp.max(lt, axis=0, keepdims=True)
    local_lse = peak + jnp.log(jnp.sum(jnp.exp(lt - peak), axis=0, keepdims=True))
    picked = jnp.sum(jnp.where(matches, lt, 0.0), axis=0, keepdims=True)
    for i in range(4):
        st_own[0, i:i + 1, :] = local_lse[:, i * 128:(i + 1) * 128]
        st_own[0, 4 + i:5 + i, :] = picked[:, i * 128:(i + 1) * 128]

    def merge(mine, others):
        every = [mine] + others
        top = functools.reduce(jnp.maximum, every)
        total = functools.reduce(jnp.add, [jnp.exp(e - top) for e in every])
        summed = functools.reduce(jnp.add, every)
        row = lax.broadcasted_iota(jnp.int32, (8, 128), 0)
        return jnp.where(row < 4, top + jnp.log(total), summed)

    copy = remote(st_own.at[0], st_core, dc=1)
    rx(copy)
    st = merge(st_own[0], [st_core[...]])
    st_own[1] = st
    group = [(i, j) for i in range(NX) for j in range(NY) if i or j]
    rx(fan([(st_own.at[1], st_xy.at[n], dict(dx=i, dy=j)) for n, (i, j) in enumerate(group)], st_xy))
    st = merge(st, [st_xy[n] for n in range(15)])
    st_own[2] = st
    rx(fan([(st_own.at[2], st_z.at[k - 1], dict(dz=k)) for k in range(1, NZ)], st_z))
    counter[0] = 0
    st = merge(st, [st_z[n] for n in range(7)])
    lse4 = st[0:4, :]
    logp4 = st[4:8, :] - lse4
    seq4 = seq_ref[...]

    def total_of(v):
        return jnp.sum(jnp.sum(v, axis=1, keepdims=True), axis=0, keepdims=True)

    seq0 = total_of(jnp.where(seq4 == 0, logp4, 0.0))
    seq1 = total_of(jnp.where(seq4 == 1, logp4, 0.0))
    margin = DPO_BETA * ((seq0 - ref_ref[0]) - (seq1 - ref_ref[1]))
    neg = jnp.broadcast_to(-margin, (8, 128))
    loss_ref[...] = jnp.maximum(neg, 0.0) + jnp.log1p(jnp.exp(-jnp.abs(neg)))
    pull = (LOSS_SCALE * DPO_BETA) / (1.0 + jnp.exp(margin))
    coef4 = jnp.where(seq4 == 0, -pull, jnp.where(seq4 == 1, pull, 0.0))
    lse = lanes(lse4)
    coef = lanes(coef4)
    lt = logits_t[...]
    g_t = coef * (matches.astype(F32) - jnp.exp(lt - lse))
    g = g_t.T.astype(BF16)
    G[...] = g

    def weight_grad(first, last):
        n = 512

        def step(i, carry):
            for k in range(4):
                at = pl.ds(pl.multiple_of(i * 4 * n + k * n, n), n)
                h = H[:, :, :, at].reshape(ROWS, n)
                dw_ref[at, :] = lax.dot_general(
                    h, G[...], (((0,), (0,)), ((), ())), preferred_element_type=F32
                ).astype(BF16)
            return carry

        lax.fori_loop(first, last, step, 0)

    def product(rows, xx, cc, off, n):
        start = pl.multiple_of((xx * 2 + cc) * 1024 + off, 128)
        return lax.dot_general(
            rows, W[pl.ds(start, n), :], (((1,), (1,)), ((), ())), preferred_element_type=F32
        )

    def x_dot(j, cc):
        return [product(G[...], wrap(x + j, NX), cc, 0, SX).reshape(NY, NZ, 16, SX)]

    def y_dot(j, cc):
        rows = G[pl.ds(pl.multiple_of(wrap(y + j, NY) * 128, 128), 128), :]
        return [product(rows, xx, cc, SX, SY).reshape(NZ, 16, SY) for xx in range(NX)]

    def z_dot(j, cc):
        p = product(G[...], j, cc, SX + SY, SZ).reshape(NY, NZ, 16, SZ)
        return [p[:, zz] for zz in range(NZ)]

    def places(part, j):
        if part == "x":
            return [(wrap(x + j, NX),)], (wrap(x + j, NX),)
        if part == "y":
            return [(wrap(y + j, NY), xx) for xx in range(NX)], (wrap(y + j, NY),)
        return [(zz, j) for zz in range(NZ)], (slice(None), j)

    parts = {"x": (x_dot, psx, plx, sx), "y": (y_dot, psy, ply, sy), "z": (z_dot, psz, plz, sz)}
    swaps = {}

    def give(part, j):
        dot, ps, land, _ = parts[part]
        idx, whole = places(part, j)
        for at, p in zip(idx, dot(j, 1 - c)):
            ps[at] = p.astype(BF16)
        swaps[part, j] = remote(ps.at[whole], land.at[whole], dc=1)

    def keep(part, j, extra=None):
        dot, _, land, s = parts[part]
        idx, _ = places(part, j)
        mine = dot(j, c)
        rx(swaps[part, j])
        for at, p in zip(idx, mine):
            s[at] = (p + land[at].astype(F32)).astype(BF16)

    def bump(ref, at, *others):
        total = ref[at].astype(F32)
        for o in others:
            total = total + o.astype(F32)
        ref[at] = total.astype(BF16)

    lo, hi = slice(0, 2), slice(2, 4)

    def send_halves(s, h, me, n, **d):
        (axis,) = d
        far = wrap(me + 2, n)
        return (
            remote(s.at[far, lo], h.at[0], **{axis: 1}),
            remote(s.at[far, hi], h.at[1], **{axis: -1}),
        )

    def near_parts(side):
        return (0, lo, hi) if side == 1 else (1, hi, lo)

    def send_near(s, land, me, n, side, axis):
        at = wrap(me + side, n)
        k, _, alone = near_parts(side)
        return remote(s.at[at, alone], land.at[k, alone], **{axis: side})

    def send_joined(s, h, land, me, n, halves_in, side, axis):
        at = wrap(me + side, n)
        k, joined, _ = near_parts(side)
        rx(halves_in[k])
        for i in (0, 1):
            bump(s, (at, 2 * k + i), h[k, i])
        return remote(s.at[at, joined], land.at[k, joined], **{axis: side})

    give("x", 2)
    give("y", 2)
    for j in range(4):
        give("z", j)
    keep("x", 2)
    xh = send_halves(sx, hx, x, NX, dx=0)
    keep("y", 2)
    yh = send_halves(sy, hy, y, NY, dy=0)
    give("x", 1)
    give("x", 3)
    for j in range(4):
        keep("z", j)

    def zat(k):
        return wrap(z + k, NZ)

    z3r = remote(sz.at[zat(3)], lz3s.at[0], dz=1)
    z3l = remote(sz.at[zat(-3)], lz3s.at[1], dz=-1)
    z4l = remote(sz.at[zat(4), lo], lz4s.at[0], dz=-2)
    z4r = remote(sz.at[zat(4), hi], lz4s.at[1], dz=2)
    z1r = remote(sz.at[zat(1)], lz1.at[0], dz=1)
    z1l = remote(sz.at[zat(-1)], lz1.at[1], dz=-1)
    keep("x", 1)
    x_in = [send_near(sx, lx1, x, NX, 1, "dx")]
    keep("x", 3)
    x_in.append(send_near(sx, lx1, x, NX, -1, "dx"))
    give("y", 1)
    give("y", 3)
    keep("y", 1)
    y_in = [send_near(sy, ly1, y, NY, 1, "dy")]
    keep("y", 3)
    y_in.append(send_near(sy, ly1, y, NY, -1, "dy"))
    give("x", 0)
    give("y", 0)
    for side in (1, -1):
        x_in.append(send_joined(sx, hx, lx1, x, NX, xh, side, "dx"))
    for side in (1, -1):
        y_in.append(send_joined(sy, hy, ly1, y, NY, yh, side, "dy"))
    keep("x", 0)
    keep("y", 0)
    rx(z3r)
    rx(z3l)
    rx(z4l)
    rx(z4r)
    for i in range(NX):
        bump(sz, (zat(-2), i), lz3s[1, i], *([lz4s[0, i]] if i < 2 else []))
    z2l = remote(sz.at[zat(-2)], lz2.at[0], dz=-2)
    for i in range(NX):
        bump(sz, (zat(2), i), lz3s[0, i], *([lz4s[1, i - 2]] if i >= 2 else []))
    z2r = remote(sz.at[zat(2)], lz2.at[1], dz=2)

    for copy in x_in:
        rx(copy)
    for yy in range(NY):
        bump(sx, (x, yy), lx1[0, yy], lx1[1, yy])
    cx = fan([(sx.at[x, wrap(y + j, NY)], lx2.at[j - 1], dict(dy=j)) for j in (1, 2, 3)], lx2)
    for copy in y_in:
        rx(copy)
    for xx in range(NX):
        bump(sy, (y, xx), ly1[0, xx], ly1[1, xx])
    cy = fan([(sy.at[y, wrap(x + j, NX)], ly2.at[j - 1], dict(dx=j)) for j in (1, 2, 3)], ly2)
    weight_grad(0, 2)
    for copy in (z1r, z1l, z2l, z2r):
        rx(copy)
    for xx in range(NX):
        bump(sz, (z, xx), lz1[0, xx], lz1[1, xx], lz2[0, xx], lz2[1, xx])
    cz = fan([(sz.at[z, wrap(x + j, NX)], lz5.at[j - 1], dict(dx=j)) for j in (1, 2, 3)], lz5)

    rx(cx)
    bump(sx, (x, y), lx2[0], lx2[1], lx2[2])
    cx = fan([(sx.at[x, y, zat(k)], lx3.at[k - 1], dict(dz=k)) for k in range(1, NZ)], lx3)
    rx(cy)
    bump(sy, (y, x), ly2[0], ly2[1], ly2[2])
    cy = fan([(sy.at[y, x, zat(k)], ly3.at[k - 1], dict(dz=k)) for k in range(1, NZ)], ly3)
    rx(cz)
    bump(sz, (z, x), lz5[0], lz5[1], lz5[2])
    cz = fan([(sz.at[z, x, wrap(y + j, NY)], lz3.at[j - 1], dict(dy=j)) for j in (1, 2, 3)], lz3)
    weight_grad(2, 4)
    rx(cx)
    total = sx[x, y, z].astype(F32)
    for k in range(7):
        total = total + lx3[k].astype(F32)
    dh_ref[:, 0:SX] = total.astype(BF16)
    rx(cy)
    total = sy[y, x, z].astype(F32)
    for k in range(7):
        total = total + ly3[k].astype(F32)
    dh_ref[:, SX:SX + SY] = total.astype(BF16)
    rx(cz)
    total = sz[z, x, y].astype(F32)
    for k in range(3):
        total = total + lz3[k].astype(F32)
    dh_ref[:, SX + SY:] = total.astype(BF16)

    drain()


def run_kernel(hidden, weight, targets, row_seq, ref_logp):
    vmem = pl.BlockSpec(memory_space=pltpu.VMEM)
    hbm = pl.BlockSpec(memory_space=pl.ANY)
    smem = pl.BlockSpec(memory_space=pltpu.SMEM)

    def v16(*shape):
        return pltpu.VMEM(shape, BF16)

    chunks = [v16(NX, NY, NZ, 16, SX), v16(NY, NX, NZ, 16, SY), v16(NZ, NX, NY, 16, SZ)]
    return pl.pallas_call(
        fused_kernel,
        out_shape=(
            pltpu.VMEM((D, VSH), BF16),
            pltpu.VMEM((8, 128), F32),
            pltpu.VMEM((16, 1024), BF16),
        ),
        in_specs=[hbm, hbm, vmem, vmem, smem],
        out_specs=(vmem, vmem, vmem),
        scratch_shapes=[
            v16(NY, NZ, 16, D),
            v16(D, VSH),
            pltpu.VMEM((NY, NZ, 16, VSH), F32),
            pltpu.VMEM((VSH, ROWS), F32),
            v16(ROWS, VSH),
            pltpu.VMEM((3, 8, 128), F32),
            pltpu.VMEM((8, 128), F32),
            pltpu.VMEM((15, 8, 128), F32),
            pltpu.VMEM((7, 8, 128), F32),
            *chunks, *chunks, *chunks,
            v16(2, 2, NZ, 16, SX), v16(2, NY, NZ, 16, SX), v16(3, NZ, 16, SX), v16(7, 16, SX),
            v16(2, 2, NZ, 16, SY), v16(2, NX, NZ, 16, SY), v16(3, NZ, 16, SY), v16(7, 16, SY),
            v16(2, NX, NY, 16, SZ), v16(2, 2, NY, 16, SZ), v16(2, NX, NY, 16, SZ),
            v16(2, NX, NY, 16, SZ), v16(3, NY, 16, SZ), v16(3, 16, SZ),
            pltpu.SemaphoreType.DMA((3,)),
            pltpu.SemaphoreType.DMA((N_SEM,)),
            pltpu.SemaphoreType.DMA((N_SEM,)),
        ],
        compiler_params=pltpu.CompilerParams(
            collective_id=0, has_side_effects=True, vmem_limit_bytes=52 * 2**20
        ),
        cost_estimate=pl.CostEstimate(flops=2 * 2 * ROWS * D * VSH, bytes_accessed=2 * D * VSH, transcendentals=0),
    )(hidden, weight, targets.reshape(4, 128), row_seq.reshape(4, 128), ref_logp)


def on_device(hidden, weight, targets, row_seq, ref_logp):
    dw, loss, dh = run_kernel(hidden, weight, targets, row_seq, ref_logp)

    def leave(dw_ref, loss_ref, dh_ref, dw_out, loss_out, dh_out, sem):
        copy = pltpu.make_async_copy(dw_ref, dw_out, sem.at[0])
        copy.start()
        loss_out[0] = loss_ref[0, 0]
        dh_out[...] = dh_ref[...]
        copy.wait()

    vmem = pl.BlockSpec(memory_space=pltpu.VMEM)
    d_weight, dpo_loss, d_hidden = pl.pallas_call(
        leave,
        out_shape=(
            jax.ShapeDtypeStruct((D, VSH), BF16),
            jax.ShapeDtypeStruct((1,), F32),
            jax.ShapeDtypeStruct((16, 1024), BF16),
        ),
        in_specs=[vmem, vmem, vmem],
        out_specs=(pl.BlockSpec(memory_space=pl.ANY), pl.BlockSpec(memory_space=pltpu.SMEM), vmem),
        scratch_shapes=[pltpu.SemaphoreType.DMA((1,))],
        compiler_params=pltpu.CompilerParams(has_side_effects=True, vmem_limit_bytes=16 * 2**20),
    )(dw, loss, dh)
    return (dpo_loss[0], d_hidden, d_weight)


def solution(mesh):
    placed = (P("ctx", None), P(None, ("ctx", "tp")), P(), P(), P())
    return jax.shard_map(
        on_device,
        mesh=mesh,
        in_specs=placed,
        out_specs=(P(), P("ctx", "tp"), P(None, ("ctx", "tp"))),
        check_vma=False,
    )
```

```python
import functools

import jax
import jax.numpy as jnp
from jax import lax
from jax.experimental import pallas as pl
from jax.experimental.pallas import tpu as pltpu
from jax.sharding import PartitionSpec as P

MESH = pl.DeviceIdType.MESH
F32 = jnp.float32
BF16 = jnp.bfloat16

DPO_BETA = 0.01
LOSS_SCALE = 1024.0

NX, NY, NZ = 4, 4, 8
ROWS = 512
D = 8192
VSH = 384
HALF = 4096

GA, GB, GQ = 1024, 1536, 384
SX, SY, SZ = 384, 384, 256

N_SEM = 53

KC = 1024


def fused_kernel(
    hid_ref, w_ref, tgt_in, seq_in, ref_in,
    dw_ref, loss_ref, dh_ref,
    H, W, L, logits_t, G,
    st_own, st_core, st_xy, st_z,
    psx, psy, psz, plx, ply, plz, sx, sy, sz,
    hx, lx1, lx2, lx3, hy, ly1, ly2, ly3, lz3s, lz4s, lz1, lz2, lz5, lz3,
    tgt_ref, seq_ref, ref_ref, local_sem, ssem, rsem,
):
    ctx = lax.axis_index("ctx")
    tp = lax.axis_index("tp")
    y = ctx // NZ
    z = lax.rem(ctx, NZ)
    x = tp // 2
    c = lax.rem(tp, 2)

    def wrap(v, n):
        return lax.rem(v + n, n)

    def dev(dy=0, dz=0, dx=0, dc=0, to_z=None):
        yy = wrap(y + dy, NY) if dy else y
        zz = wrap(z + dz, NZ) if dz else z
        zz = zz if to_z is None else to_z
        xx = wrap(x + dx, NX) if dx else x
        cc = 1 - c if dc else c
        return (yy * NZ + zz, xx * 2 + cc)

    counter = [0]
    sends = []

    def number():
        counter[0] += 1
        return counter[0] - 1

    def remote(src, dst, i=None, **d):
        i_own = number() if i is None else i
        copy = pltpu.make_async_remote_copy(
            src_ref=src, dst_ref=dst, send_sem=ssem.at[i_own], recv_sem=rsem.at[i_own],
            device_id=dev(**d), device_id_type=MESH,
        )
        copy.start()
        if i is None:
            sends.append(copy)
            return copy

    def all_of(i, whole, **d):
        copy = pltpu.make_async_remote_copy(
            src_ref=whole, dst_ref=whole, send_sem=ssem.at[i], recv_sem=rsem.at[i],
            device_id=dev(**d), device_id_type=MESH,
        )
        sends.append(copy)
        return copy

    def fan(pairs, whole):
        i = number()
        for src, dst, d in pairs:
            remote(src, dst, i, **d)
        return all_of(i, whole, **pairs[0][2])

    def rx(copy):
        copy.wait_recv()

    def drain():
        for copy in sends:
            copy.wait_send()
        sends.clear()

    c0 = c * HALF
    col_a = pl.multiple_of(c0, 128)
    col_b = pl.multiple_of(c0 + GA, 128)
    col_q0 = pl.multiple_of(c0 + GA + GB, 128)
    col_q = pl.multiple_of(c0 + GA + GB + x * GQ, 128)

    w_load = pltpu.make_async_copy(w_ref, W, local_sem.at[0])
    w_load.start()
    own_ab = pltpu.make_async_copy(
        hid_ref.at[:, pl.ds(col_a, GA + GB)], H.at[y, z, :, pl.ds(col_a, GA + GB)], local_sem.at[1]
    )
    own_ab.start()
    own_q = pltpu.make_async_copy(
        hid_ref.at[:, pl.ds(col_q, GQ)], H.at[y, z, :, pl.ds(col_q, GQ)], local_sem.at[2]
    )
    own_q.start()

    small = [
        pltpu.make_async_copy(src, dst, local_sem.at[3 + n])
        for n, (src, dst) in enumerate(((tgt_in, tgt_ref), (seq_in, seq_ref), (ref_in, ref_ref)))
    ]
    for copy in small:
        copy.start()

    barrier = pltpu.get_barrier_semaphore()
    peers = [dict(dc=1)]
    peers += [dict(dx=i, dy=j) for i in range(NX) for j in range(NY) if i or j]
    peers += [dict(dz=k) for k in range(1, NZ)]
    for p in peers:
        pl.semaphore_signal(barrier, inc=1, device_id=dev(**p), device_id_type=MESH)
    pl.semaphore_wait(barrier, len(peers))
    for copy in small:
        copy.wait()
    own_ab.wait()
    own_q.wait()

    def blk_a(zz):
        return H.at[:, zz, :, pl.ds(col_a, GA)]

    def blk_b(yy, zz):
        return H.at[yy, zz, :, pl.ds(col_b, GB)]

    def blk_q(zz):
        return H.at[:, zz, :, pl.ds(col_q, GQ)]

    own_a = H.at[y, z, :, pl.ds(col_a, GA)]
    own_qb = H.at[y, z, :, pl.ds(col_q, GQ)]
    first_a = fan([(own_a, own_a, dict(dy=j)) for j in (1, 2, 3)], H.at[0:3, z, :, pl.ds(col_a, GA)])
    first_q = fan([(own_qb, own_qb, dict(dy=j)) for j in (1, 2, 3)], H.at[0:3, z, :, pl.ds(col_q, GQ)])

    def both_ways(ref):
        return (remote(ref, ref, dz=1), remote(ref, ref, dz=-1))

    def fan_y(zz):
        ref = blk_b(y, zz)
        return fan([(ref, ref, dict(dy=j)) for j in (1, 2, 3)], H.at[0:3, zz, :, pl.ds(col_b, GB)])

    def fan_x(zz):
        ref = blk_q(zz)
        return fan([(ref, ref, dict(dx=j)) for j in (1, 2, 3)], H.at[:, zz, :, pl.ds(col_q0, 3 * GQ)])

    handed = {}
    arrivals = {}

    def hand_over(key, ref):
        if key not in handed:
            handed[key] = number()
        remote(ref, ref, handed[key], dc=1)

    def hand_on(key, zz):
        from_y, from_x = arrivals.pop(key)
        rx(from_y)
        hand_over(key, H.at[:, zz, :, pl.ds(col_b, GB)])
        rx(from_x)
        hand_over(key, H.at[:, zz, :, pl.ds(col_q0, NX * GQ)])
        handed[key] = all_of(handed[key], H.at[:, zz, :, pl.ds(col_a, HALF)], dc=1)

    def logits_of(keys):
        zs = [wrap(z - sign * st, NZ) for st, sign in keys]
        for key in keys:
            rx(handed[key])
        acc = jnp.zeros((64 * len(zs), VSH), F32)
        for k in range(0, D, KC):
            h = jnp.concatenate([H[yy, zz, :, k:k + KC] for zz in zs for yy in range(NY)], axis=0)
            acc = acc + jnp.dot(h, W[k:k + KC, :], preferred_element_type=F32)
        acc = acc.reshape(len(zs), NY, 16, VSH)
        for n, zz in enumerate(zs):
            L[:, zz] = acc[n]

    ring_b = both_ways(blk_b(y, z))
    fy = fan_y(z)
    rx(first_a)
    ring_a = both_ways(blk_a(z))
    rx(first_q)
    ring_q = both_ways(blk_q(z))
    fx = fan_x(z)
    hand_over((0, 1), blk_a(z))
    arrivals[0, 1] = (fy, fx)

    def halves(yy, zz, col, n, k):
        cut = n // 256 * 128
        lo = col if k == 0 else pl.multiple_of(col + cut, 128)
        return H.at[yy, zz, :, pl.ds(lo, cut if k == 0 else n - cut)]

    for s in (1, 2, 3):
        nb, na, nq = [], [], []
        for k, sign in ((0, 1), (1, -1)):
            zz = wrap(z - sign * s, NZ)
            rx(ring_b[k])
            ref = blk_b(y, zz) if s < 3 else halves(y, zz, col_b, GB, k)
            nb.append(remote(ref, ref, dz=sign))
            fy = fan_y(zz)
            rx(ring_q[k])
            ref = blk_q(zz) if s < 3 else halves(slice(None), zz, col_q, GQ, k)
            nq.append(remote(ref, ref, dz=sign))
            fx = fan_x(zz)
            rx(ring_a[k])
            ref = blk_a(zz) if s < 3 else halves(slice(None), zz, col_a, GA, k)
            na.append(remote(ref, ref, dz=sign))
            hand_over((s, sign), blk_a(zz))
            arrivals[s, sign] = (fy, fx)
        for key in list(arrivals):
            if key[0] < s:
                hand_on(key, wrap(z - key[1] * key[0], NZ))
        if s == 2:
            w_load.wait()
        if s == 3:
            logits_of([(1, 1), (1, -1)])
        ring_b, ring_a, ring_q = nb, na, nq

    zz = wrap(z + 4, NZ)
    rx(ring_b[0])
    rx(ring_b[1])
    fy = fan_y(zz)
    rx(ring_q[0])
    rx(ring_q[1])
    fx = fan_x(zz)
    rx(ring_a[0])
    rx(ring_a[1])
    hand_over((4, -1), blk_a(zz))
    arrivals[4, -1] = (fy, fx)
    hand_on((3, 1), wrap(z - 3, NZ))
    hand_on((3, -1), wrap(z + 3, NZ))
    logits_of([(2, 1), (2, -1)])
    hand_on((4, -1), zz)
    logits_of([(3, 1), (3, -1)])
    logits_of([(0, 1), (4, -1)])
    drain()

    lt = L[...].reshape(ROWS, VSH).T
    logits_t[...] = lt

    def lanes(ref4):
        return jnp.concatenate([ref4[i:i + 1, :] for i in range(4)], axis=1)

    targets = lanes(tgt_ref[...])
    first_col = (ctx * 8 + tp) * VSH
    cols = first_col + lax.broadcasted_iota(jnp.int32, (VSH, ROWS), 0)
    matches = cols == targets
    peak = jnp.max(lt, axis=0, keepdims=True)
    local_lse = peak + jnp.log(jnp.sum(jnp.exp(lt - peak), axis=0, keepdims=True))
    picked = jnp.sum(jnp.where(matches, lt, 0.0), axis=0, keepdims=True)
    for i in range(4):
        st_own[0, i:i + 1, :] = local_lse[:, i * 128:(i + 1) * 128]
        st_own[0, 4 + i:5 + i, :] = picked[:, i * 128:(i + 1) * 128]

    def merge(mine, others):
        every = [mine] + others
        top = functools.reduce(jnp.maximum, every)
        total = functools.reduce(jnp.add, [jnp.exp(e - top) for e in every])
        summed = functools.reduce(jnp.add, every)
        row = lax.broadcasted_iota(jnp.int32, (8, 128), 0)
        return jnp.where(row < 4, top + jnp.log(total), summed)

    copy = remote(st_own.at[0], st_core, dc=1)
    rx(copy)
    st = merge(st_own[0], [st_core[...]])
    st_own[1] = st
    group = [(i, j) for i in range(NX) for j in range(NY) if i or j]
    rx(fan([(st_own.at[1], st_xy.at[n], dict(dx=i, dy=j)) for n, (i, j) in enumerate(group)], st_xy))
    st = merge(st, [st_xy[n] for n in range(15)])
    st_own[2] = st
    rx(fan([(st_own.at[2], st_z.at[k - 1], dict(dz=k)) for k in range(1, NZ)], st_z))
    counter[0] = 0
    st = merge(st, [st_z[n] for n in range(7)])
    lse4 = st[0:4, :]
    logp4 = st[4:8, :] - lse4
    seq4 = seq_ref[...]

    def total_of(v):
        return jnp.sum(jnp.sum(v, axis=1, keepdims=True), axis=0, keepdims=True)

    seq0 = total_of(jnp.where(seq4 == 0, logp4, 0.0))
    seq1 = total_of(jnp.where(seq4 == 1, logp4, 0.0))
    margin = DPO_BETA * ((seq0 - ref_ref[:, 0:1]) - (seq1 - ref_ref[:, 1:2]))
    neg = jnp.broadcast_to(-margin, (8, 128))
    loss_ref[...] = jnp.maximum(neg, 0.0) + jnp.log1p(jnp.exp(-jnp.abs(neg)))
    pull = (LOSS_SCALE * DPO_BETA) / (1.0 + jnp.exp(margin))
    coef4 = jnp.where(seq4 == 0, -pull, jnp.where(seq4 == 1, pull, 0.0))
    lse = lanes(lse4)
    coef = lanes(coef4)
    lt = logits_t[...]
    g_t = coef * (matches.astype(F32) - jnp.exp(lt - lse))
    g = g_t.T.astype(BF16)
    G[...] = g

    def weight_grad(first, last):
        n = 512

        def step(i, carry):
            for k in range(4):
                at = pl.ds(pl.multiple_of(i * 4 * n + k * n, n), n)
                h = H[:, :, :, at].reshape(ROWS, n)
                dw_ref[at, :] = lax.dot_general(
                    h, G[...], (((0,), (0,)), ((), ())), preferred_element_type=F32
                ).astype(BF16)
            return carry

        lax.fori_loop(first, last, step, 0)

    def product(rows, xx, cc, off, n):
        start = pl.multiple_of((xx * 2 + cc) * 1024 + off, 128)
        return lax.dot_general(
            rows, W[pl.ds(start, n), :], (((1,), (1,)), ((), ())), preferred_element_type=F32
        )

    def x_dot(j, cc):
        return [product(G[...], wrap(x + j, NX), cc, 0, SX).reshape(NY, NZ, 16, SX)]

    def y_dot(j, cc):
        rows = G[pl.ds(pl.multiple_of(wrap(y + j, NY) * 128, 128), 128), :]
        return [product(rows, xx, cc, SX, SY).reshape(NZ, 16, SY) for xx in range(NX)]

    def z_dot(j, cc):
        p = product(G[...], j, cc, SX + SY, SZ).reshape(NY, NZ, 16, SZ)
        return [p[:, zz] for zz in range(NZ)]

    def places(part, j):
        if part == "x":
            return [(wrap(x + j, NX),)], (wrap(x + j, NX),)
        if part == "y":
            return [(wrap(y + j, NY), xx) for xx in range(NX)], (wrap(y + j, NY),)
        return [(zz, j) for zz in range(NZ)], (slice(None), j)

    parts = {"x": (x_dot, psx, plx, sx), "y": (y_dot, psy, ply, sy), "z": (z_dot, psz, plz, sz)}
    swaps = {}

    def give(part, j):
        dot, ps, land, _ = parts[part]
        idx, whole = places(part, j)
        for at, p in zip(idx, dot(j, 1 - c)):
            ps[at] = p.astype(BF16)
        swaps[part, j] = remote(ps.at[whole], land.at[whole], dc=1)

    def keep(part, j, extra=None):
        dot, _, land, s = parts[part]
        idx, _ = places(part, j)
        mine = dot(j, c)
        rx(swaps[part, j])
        for at, p in zip(idx, mine):
            s[at] = (p + land[at].astype(F32)).astype(BF16)

    def bump(ref, at, *others):
        total = ref[at].astype(F32)
        for o in others:
            total = total + o.astype(F32)
        ref[at] = total.astype(BF16)

    lo, hi = slice(0, 2), slice(2, 4)

    def send_halves(s, h, me, n, **d):
        (axis,) = d
        far = wrap(me + 2, n)
        return (
            remote(s.at[far, lo], h.at[0], **{axis: 1}),
            remote(s.at[far, hi], h.at[1], **{axis: -1}),
        )

    def near_parts(side):
        return (0, lo, hi) if side == 1 else (1, hi, lo)

    def send_near(s, land, me, n, side, axis):
        at = wrap(me + side, n)
        k, _, alone = near_parts(side)
        return remote(s.at[at, alone], land.at[k, alone], **{axis: side})

    def send_joined(s, h, land, me, n, halves_in, side, axis):
        at = wrap(me + side, n)
        k, joined, _ = near_parts(side)
        rx(halves_in[k])
        for i in (0, 1):
            bump(s, (at, 2 * k + i), h[k, i])
        return remote(s.at[at, joined], land.at[k, joined], **{axis: side})

    give("x", 2)
    give("y", 2)
    for j in range(4):
        give("z", j)
    keep("x", 2)
    xh = send_halves(sx, hx, x, NX, dx=0)
    keep("y", 2)
    yh = send_halves(sy, hy, y, NY, dy=0)
    give("x", 1)
    give("x", 3)
    for j in range(4):
        keep("z", j)

    def zat(k):
        return wrap(z + k, NZ)

    z3r = remote(sz.at[zat(3)], lz3s.at[0], dz=1)
    z3l = remote(sz.at[zat(-3)], lz3s.at[1], dz=-1)
    z4l = remote(sz.at[zat(4), lo], lz4s.at[0], dz=-2)
    z4r = remote(sz.at[zat(4), hi], lz4s.at[1], dz=2)
    z1r = remote(sz.at[zat(1)], lz1.at[0], dz=1)
    z1l = remote(sz.at[zat(-1)], lz1.at[1], dz=-1)
    keep("x", 1)
    x_in = [send_near(sx, lx1, x, NX, 1, "dx")]
    keep("x", 3)
    x_in.append(send_near(sx, lx1, x, NX, -1, "dx"))
    give("y", 1)
    give("y", 3)
    keep("y", 1)
    y_in = [send_near(sy, ly1, y, NY, 1, "dy")]
    keep("y", 3)
    y_in.append(send_near(sy, ly1, y, NY, -1, "dy"))
    give("x", 0)
    give("y", 0)
    for side in (1, -1):
        x_in.append(send_joined(sx, hx, lx1, x, NX, xh, side, "dx"))
    for side in (1, -1):
        y_in.append(send_joined(sy, hy, ly1, y, NY, yh, side, "dy"))
    keep("x", 0)
    keep("y", 0)
    rx(z3r)
    rx(z3l)
    rx(z4l)
    rx(z4r)
    for i in range(NX):
        bump(sz, (zat(-2), i), lz3s[1, i], *([lz4s[0, i]] if i < 2 else []))
    z2l = remote(sz.at[zat(-2)], lz2.at[0], dz=-2)
    for i in range(NX):
        bump(sz, (zat(2), i), lz3s[0, i], *([lz4s[1, i - 2]] if i >= 2 else []))
    z2r = remote(sz.at[zat(2)], lz2.at[1], dz=2)

    far, near = (1 - z // 4) * 4, z // 4 * 4

    def second(s, a, b, n, land, axis):
        return [
            fan(
                [
                    (s.at[a, wrap(b + j, n), pl.ds(h, 4)], land.at[j - 1, pl.ds(h, 4)], {axis: j})
                    for j in (1, 2, 3)
                ],
                land.at[:, pl.ds(h, 4)],
            )
            for h in (far, near)
        ]

    def third(s, a, b, land, out, first):
        h = far if first else near
        bump(s, (a, b, pl.ds(h, 4)), *[land[j, pl.ds(h, 4)] for j in range(3)])
        to = [far + i for i in range(4)] if first else [near + lax.rem(z + k, 4) for k in (1, 2, 3)]
        return fan([(s.at[a, b, zz], out.at[z], dict(to_z=zz)) for zz in to], out.at[0:len(to)])

    for copy in x_in:
        rx(copy)
    for yy in range(NY):
        bump(sx, (x, yy), lx1[0, yy], lx1[1, yy])
    cx = second(sx, x, y, NY, lx2, "dy")
    for copy in y_in:
        rx(copy)
    for xx in range(NX):
        bump(sy, (y, xx), ly1[0, xx], ly1[1, xx])
    cy = second(sy, y, x, NX, ly2, "dx")
    weight_grad(0, 2)
    for copy in (z1r, z1l, z2l, z2r):
        rx(copy)
    for xx in range(NX):
        bump(sz, (z, xx), lz1[0, xx], lz1[1, xx], lz2[0, xx], lz2[1, xx])
    cz = fan([(sz.at[z, wrap(x + j, NX)], lz5.at[j - 1], dict(dx=j)) for j in (1, 2, 3)], lz5)

    rx(cx[0])
    cx[0] = third(sx, x, y, lx2, lx3, True)
    rx(cy[0])
    cy[0] = third(sy, y, x, ly2, ly3, True)
    rx(cx[1])
    cx[1] = third(sx, x, y, lx2, lx3, False)
    rx(cy[1])
    cy[1] = third(sy, y, x, ly2, ly3, False)
    rx(cz)
    bump(sz, (z, x), lz5[0], lz5[1], lz5[2])
    cz = fan([(sz.at[z, x, wrap(y + j, NY)], lz3.at[j - 1], dict(dy=j)) for j in (1, 2, 3)], lz3)
    weight_grad(2, 4)
    rx(cx[0])
    rx(cx[1])
    total = sx[x, y, z].astype(F32)
    for k in range(1, NZ):
        total = total + lx3[zat(k)].astype(F32)
    dh_ref[:, 0:SX] = total.astype(BF16)
    rx(cy[0])
    rx(cy[1])
    total = sy[y, x, z].astype(F32)
    for k in range(1, NZ):
        total = total + ly3[zat(k)].astype(F32)
    dh_ref[:, SX:SX + SY] = total.astype(BF16)
    rx(cz)
    total = sz[z, x, y].astype(F32)
    for k in range(3):
        total = total + lz3[k].astype(F32)
    dh_ref[:, SX + SY:] = total.astype(BF16)

    drain()


def run_kernel(hidden, weight, targets, row_seq, ref_logp):
    vmem = pl.BlockSpec(memory_space=pltpu.VMEM)
    hbm = pl.BlockSpec(memory_space=pl.ANY)

    def v16(*shape):
        return pltpu.VMEM(shape, BF16)

    chunks = [v16(NX, NY, NZ, 16, SX), v16(NY, NX, NZ, 16, SY), v16(NZ, NX, NY, 16, SZ)]
    return pl.pallas_call(
        fused_kernel,
        out_shape=(
            pltpu.VMEM((D, VSH), BF16),
            pltpu.VMEM((8, 128), F32),
            pltpu.VMEM((16, 1024), BF16),
        ),
        in_specs=[hbm] * 5,
        out_specs=(vmem, vmem, vmem),
        scratch_shapes=[
            v16(NY, NZ, 16, D),
            v16(D, VSH),
            pltpu.VMEM((NY, NZ, 16, VSH), F32),
            pltpu.VMEM((VSH, ROWS), F32),
            v16(ROWS, VSH),
            pltpu.VMEM((3, 8, 128), F32),
            pltpu.VMEM((8, 128), F32),
            pltpu.VMEM((15, 8, 128), F32),
            pltpu.VMEM((7, 8, 128), F32),
            *chunks, *chunks, *chunks,
            v16(2, 2, NZ, 16, SX), v16(2, NY, NZ, 16, SX), v16(3, NZ, 16, SX), v16(NZ, 16, SX),
            v16(2, 2, NZ, 16, SY), v16(2, NX, NZ, 16, SY), v16(3, NZ, 16, SY), v16(NZ, 16, SY),
            v16(2, NX, NY, 16, SZ), v16(2, 2, NY, 16, SZ), v16(2, NX, NY, 16, SZ),
            v16(2, NX, NY, 16, SZ), v16(3, NY, 16, SZ), v16(3, 16, SZ),
            pltpu.VMEM((4, 128), jnp.int32), pltpu.VMEM((4, 128), jnp.int32), pltpu.VMEM((1, 2), F32),
            pltpu.SemaphoreType.DMA((6,)),
            pltpu.SemaphoreType.DMA((N_SEM,)),
            pltpu.SemaphoreType.DMA((N_SEM,)),
        ],
        compiler_params=pltpu.CompilerParams(
            collective_id=0, has_side_effects=True, vmem_limit_bytes=52 * 2**20
        ),
        cost_estimate=pl.CostEstimate(flops=2 * 2 * ROWS * D * VSH, bytes_accessed=2 * D * VSH, transcendentals=0),
    )(hidden, weight, targets.reshape(4, 128), row_seq.reshape(4, 128), ref_logp.reshape(1, 2))


def on_device(hidden, weight, targets, row_seq, ref_logp):
    dw, loss, dh = run_kernel(hidden, weight, targets, row_seq, ref_logp)

    def leave(dw_ref, loss_ref, dh_ref, dw_out, loss_out, dh_out, sem):
        copy = pltpu.make_async_copy(dw_ref, dw_out, sem.at[0])
        copy.start()
        loss_out[0] = loss_ref[0, 0]
        dh_out[...] = dh_ref[...]
        copy.wait()

    vmem = pl.BlockSpec(memory_space=pltpu.VMEM)
    d_weight, dpo_loss, d_hidden = pl.pallas_call(
        leave,
        out_shape=(
            jax.ShapeDtypeStruct((D, VSH), BF16),
            jax.ShapeDtypeStruct((1,), F32),
            jax.ShapeDtypeStruct((16, 1024), BF16),
        ),
        in_specs=[vmem, vmem, vmem],
        out_specs=(pl.BlockSpec(memory_space=pl.ANY), pl.BlockSpec(memory_space=pltpu.SMEM), vmem),
        scratch_shapes=[pltpu.SemaphoreType.DMA((1,))],
        compiler_params=pltpu.CompilerParams(has_side_effects=True, vmem_limit_bytes=16 * 2**20),
    )(dw, loss, dh)
    return (dpo_loss[0], d_hidden, d_weight)


def solution(mesh):
    placed = (P("ctx", None), P(None, ("ctx", "tp")), P(), P(), P())
    return jax.shard_map(
        on_device,
        mesh=mesh,
        in_specs=placed,
        out_specs=(P(), P("ctx", "tp"), P(None, ("ctx", "tp"))),
        check_vma=False,
    )
```

```python
import functools

import jax
import jax.numpy as jnp
from jax import lax
from jax.experimental import pallas as pl
from jax.experimental.pallas import tpu as pltpu
from jax.sharding import PartitionSpec as P

MESH = pl.DeviceIdType.MESH
F32 = jnp.float32
BF16 = jnp.bfloat16

DPO_BETA = 0.01
LOSS_SCALE = 1024.0

NX, NY, NZ = 4, 4, 8
ROWS = 512
D = 8192
VSH = 384
HALF = 4096

GA, GB, GQ = 1024, 1536, 384
SX, SY, SZ = 384, 384, 256

N_SEM = 53

KC = 1024


def fused_kernel(
    hid_ref, w_ref, tgt_in, seq_in, ref_in,
    dw_ref, loss_ref, dh_ref,
    H, W, L, logits_t, G,
    st_own, st_core, st_xy, st_z,
    psx, psy, psz, plx, ply, plz, sx, sy, sz,
    hx, lx1, lx2, lx3, hy, ly1, ly2, ly3, lz3s, lz4s, lz1, lz2, lz5, lz3,
    tgt_ref, seq_ref, ref_ref, local_sem, ssem, rsem,
):
    ctx = lax.axis_index("ctx")
    tp = lax.axis_index("tp")
    y = ctx // NZ
    z = lax.rem(ctx, NZ)
    x = tp // 2
    c = lax.rem(tp, 2)

    def wrap(v, n):
        return lax.rem(v + n, n)

    def dev(dy=0, dz=0, dx=0, dc=0, to_z=None):
        yy = wrap(y + dy, NY) if dy else y
        zz = wrap(z + dz, NZ) if dz else z
        zz = zz if to_z is None else to_z
        xx = wrap(x + dx, NX) if dx else x
        cc = 1 - c if dc else c
        return (yy * NZ + zz, xx * 2 + cc)

    counter = [0]
    sends = []

    def number():
        counter[0] += 1
        return counter[0] - 1

    def remote(src, dst, i=None, **d):
        i_own = number() if i is None else i
        copy = pltpu.make_async_remote_copy(
            src_ref=src, dst_ref=dst, send_sem=ssem.at[i_own], recv_sem=rsem.at[i_own],
            device_id=dev(**d), device_id_type=MESH,
        )
        copy.start()
        if i is None:
            sends.append(copy)
            return copy

    def all_of(i, whole, **d):
        copy = pltpu.make_async_remote_copy(
            src_ref=whole, dst_ref=whole, send_sem=ssem.at[i], recv_sem=rsem.at[i],
            device_id=dev(**d), device_id_type=MESH,
        )
        sends.append(copy)
        return copy

    def fan(pairs, whole):
        i = number()
        for src, dst, d in pairs:
            remote(src, dst, i, **d)
        return all_of(i, whole, **pairs[0][2])

    def rx(copy):
        copy.wait_recv()

    def drain():
        for copy in sends:
            copy.wait_send()
        sends.clear()

    c0 = c * HALF
    col_a = pl.multiple_of(c0, 128)
    col_b = pl.multiple_of(c0 + GA, 128)
    col_q0 = pl.multiple_of(c0 + GA + GB, 128)
    col_q = pl.multiple_of(c0 + GA + GB + x * GQ, 128)

    w_load = pltpu.make_async_copy(w_ref, W, local_sem.at[0])
    w_load.start()
    own_ab = pltpu.make_async_copy(
        hid_ref.at[:, pl.ds(col_a, GA + GB)], H.at[y, z, :, pl.ds(col_a, GA + GB)], local_sem.at[1]
    )
    own_ab.start()
    own_q = pltpu.make_async_copy(
        hid_ref.at[:, pl.ds(col_q, GQ)], H.at[y, z, :, pl.ds(col_q, GQ)], local_sem.at[2]
    )
    own_q.start()

    small = [
        pltpu.make_async_copy(src, dst, local_sem.at[3 + n])
        for n, (src, dst) in enumerate(((tgt_in, tgt_ref), (seq_in, seq_ref), (ref_in, ref_ref)))
    ]
    for copy in small:
        copy.start()

    barrier = pltpu.get_barrier_semaphore()
    plane = [(i, j) for i in range(NX) for j in range(NY) if i or j]
    plane.sort(key=lambda p: -min(p[0], NX - p[0]) - min(p[1], NY - p[1]))
    line = sorted(range(1, NZ), key=lambda k: -min(k, NZ - k))
    peers = [dict(dx=i, dy=j) for i, j in plane] + [dict(dz=k) for k in line] + [dict(dc=1)]
    for p in peers:
        pl.semaphore_signal(barrier, inc=1, device_id=dev(**p), device_id_type=MESH)
    pl.semaphore_wait(barrier, len(peers))
    for copy in small:
        copy.wait()
    own_ab.wait()
    own_q.wait()

    def blk_a(zz):
        return H.at[:, zz, :, pl.ds(col_a, GA)]

    def blk_b(yy, zz):
        return H.at[yy, zz, :, pl.ds(col_b, GB)]

    def blk_q(zz):
        return H.at[:, zz, :, pl.ds(col_q, GQ)]

    own_a = H.at[y, z, :, pl.ds(col_a, GA)]
    own_qb = H.at[y, z, :, pl.ds(col_q, GQ)]
    first_a = fan([(own_a, own_a, dict(dy=j)) for j in (1, 2, 3)], H.at[0:3, z, :, pl.ds(col_a, GA)])
    first_q = fan([(own_qb, own_qb, dict(dy=j)) for j in (1, 2, 3)], H.at[0:3, z, :, pl.ds(col_q, GQ)])

    def both_ways(ref):
        return (remote(ref, ref, dz=1), remote(ref, ref, dz=-1))

    def fan_y(zz):
        ref = blk_b(y, zz)
        return fan([(ref, ref, dict(dy=j)) for j in (1, 2, 3)], H.at[0:3, zz, :, pl.ds(col_b, GB)])

    def fan_x(zz):
        ref = blk_q(zz)
        return fan([(ref, ref, dict(dx=j)) for j in (1, 2, 3)], H.at[:, zz, :, pl.ds(col_q0, 3 * GQ)])

    handed = {}
    arrivals = {}

    def hand_over(key, ref):
        if key not in handed:
            handed[key] = number()
        remote(ref, ref, handed[key], dc=1)

    def hand_on(key, zz):
        from_y, from_x = arrivals.pop(key)
        rx(from_y)
        hand_over(key, H.at[:, zz, :, pl.ds(col_b, GB)])
        rx(from_x)
        hand_over(key, H.at[:, zz, :, pl.ds(col_q0, NX * GQ)])
        handed[key] = all_of(handed[key], H.at[:, zz, :, pl.ds(col_a, HALF)], dc=1)

    def logits_of(keys):
        zs = [wrap(z - sign * st, NZ) for st, sign in keys]
        for key in keys:
            rx(handed[key])
        acc = jnp.zeros((64 * len(zs), VSH), F32)
        for k in range(0, D, KC):
            h = jnp.concatenate([H[yy, zz, :, k:k + KC] for zz in zs for yy in range(NY)], axis=0)
            acc = acc + jnp.dot(h, W[k:k + KC, :], preferred_element_type=F32)
        acc = acc.reshape(len(zs), NY, 16, VSH)
        for n, zz in enumerate(zs):
            L[:, zz] = acc[n]

    ring_b = both_ways(blk_b(y, z))
    fy = fan_y(z)
    rx(first_a)
    ring_a = both_ways(blk_a(z))
    rx(first_q)
    ring_q = both_ways(blk_q(z))
    fx = fan_x(z)
    hand_over((0, 1), blk_a(z))
    arrivals[0, 1] = (fy, fx)

    def halves(yy, zz, col, n, k):
        cut = n // 256 * 128
        lo = col if k == 0 else pl.multiple_of(col + cut, 128)
        return H.at[yy, zz, :, pl.ds(lo, cut if k == 0 else n - cut)]

    for s in (1, 2, 3):
        nb, na, nq = [], [], []
        for k, sign in ((0, 1), (1, -1)):
            zz = wrap(z - sign * s, NZ)
            rx(ring_b[k])
            ref = blk_b(y, zz) if s < 3 else halves(y, zz, col_b, GB, k)
            nb.append(remote(ref, ref, dz=sign))
            fy = fan_y(zz)
            rx(ring_q[k])
            ref = blk_q(zz) if s < 3 else halves(slice(None), zz, col_q, GQ, k)
            nq.append(remote(ref, ref, dz=sign))
            fx = fan_x(zz)
            rx(ring_a[k])
            ref = blk_a(zz) if s < 3 else halves(slice(None), zz, col_a, GA, k)
            na.append(remote(ref, ref, dz=sign))
            hand_over((s, sign), blk_a(zz))
            arrivals[s, sign] = (fy, fx)
        for key in list(arrivals):
            if key[0] < s:
                hand_on(key, wrap(z - key[1] * key[0], NZ))
        if s == 2:
            w_load.wait()
        if s == 3:
            logits_of([(1, 1), (1, -1)])
        ring_b, ring_a, ring_q = nb, na, nq

    zz = wrap(z + 4, NZ)
    rx(ring_b[0])
    rx(ring_b[1])
    fy = fan_y(zz)
    rx(ring_q[0])
    rx(ring_q[1])
    fx = fan_x(zz)
    rx(ring_a[0])
    rx(ring_a[1])
    hand_over((4, -1), blk_a(zz))
    arrivals[4, -1] = (fy, fx)
    hand_on((3, 1), wrap(z - 3, NZ))
    hand_on((3, -1), wrap(z + 3, NZ))
    logits_of([(2, 1), (2, -1)])
    hand_on((4, -1), zz)
    logits_of([(3, 1), (3, -1)])
    logits_of([(0, 1), (4, -1)])

    lt = L[...].reshape(ROWS, VSH).T
    logits_t[...] = lt

    def lanes(ref4):
        return jnp.concatenate([ref4[i:i + 1, :] for i in range(4)], axis=1)

    targets = lanes(tgt_ref[...])
    first_col = (ctx * 8 + tp) * VSH
    cols = first_col + lax.broadcasted_iota(jnp.int32, (VSH, ROWS), 0)
    matches = cols == targets
    peak = jnp.max(lt, axis=0, keepdims=True)
    local_lse = peak + jnp.log(jnp.sum(jnp.exp(lt - peak), axis=0, keepdims=True))
    picked = jnp.sum(jnp.where(matches, lt, 0.0), axis=0, keepdims=True)
    for i in range(4):
        st_own[0, i:i + 1, :] = local_lse[:, i * 128:(i + 1) * 128]
        st_own[0, 4 + i:5 + i, :] = picked[:, i * 128:(i + 1) * 128]

    def merge(mine, others):
        every = [mine] + others
        top = functools.reduce(jnp.maximum, every)
        total = functools.reduce(jnp.add, [jnp.exp(e - top) for e in every])
        summed = functools.reduce(jnp.add, every)
        row = lax.broadcasted_iota(jnp.int32, (8, 128), 0)
        return jnp.where(row < 4, top + jnp.log(total), summed)

    copy = remote(st_own.at[0], st_core, dc=1)
    rx(copy)
    st = merge(st_own[0], [st_core[...]])
    st_own[1] = st
    gathered = sends[:]
    sends.clear()
    copy = fan([(st_own.at[1], st_xy.at[n], dict(dx=i, dy=j)) for n, (i, j) in enumerate(plane)], st_xy)
    for earlier in gathered:
        earlier.wait_send()
    rx(copy)
    st = merge(st, [st_xy[n] for n in range(15)])
    st_own[2] = st
    rx(fan([(st_own.at[2], st_z.at[n], dict(dz=k)) for n, k in enumerate(line)], st_z))
    drain()
    counter[0] = 0
    st = merge(st, [st_z[n] for n in range(7)])
    lse4 = st[0:4, :]
    logp4 = st[4:8, :] - lse4
    seq4 = seq_ref[...]

    def total_of(v):
        return jnp.sum(jnp.sum(v, axis=1, keepdims=True), axis=0, keepdims=True)

    seq0 = total_of(jnp.where(seq4 == 0, logp4, 0.0))
    seq1 = total_of(jnp.where(seq4 == 1, logp4, 0.0))
    margin = DPO_BETA * ((seq0 - ref_ref[:, 0:1]) - (seq1 - ref_ref[:, 1:2]))
    neg = jnp.broadcast_to(-margin, (8, 128))
    loss_ref[...] = jnp.maximum(neg, 0.0) + jnp.log1p(jnp.exp(-jnp.abs(neg)))
    pull = (LOSS_SCALE * DPO_BETA) / (1.0 + jnp.exp(margin))
    coef4 = jnp.where(seq4 == 0, -pull, jnp.where(seq4 == 1, pull, 0.0))
    lse = lanes(lse4)
    coef = lanes(coef4)
    lt = logits_t[...]
    g_t = coef * (matches.astype(F32) - jnp.exp(lt - lse))
    g = g_t.T.astype(BF16)
    G[...] = g

    def weight_grad(first, last):
        n = 512

        def step(i, carry):
            for k in range(4):
                at = pl.ds(pl.multiple_of(i * 4 * n + k * n, n), n)
                h = H[:, :, :, at].reshape(ROWS, n)
                dw_ref[at, :] = lax.dot_general(
                    h, G[...], (((0,), (0,)), ((), ())), preferred_element_type=F32
                ).astype(BF16)
            return carry

        lax.fori_loop(first, last, step, 0)

    def product(rows, xx, cc, off, n):
        start = pl.multiple_of((xx * 2 + cc) * 1024 + off, 128)
        return lax.dot_general(
            rows, W[pl.ds(start, n), :], (((1,), (1,)), ((), ())), preferred_element_type=F32
        )

    def x_dot(j, cc):
        return [product(G[...], wrap(x + j, NX), cc, 0, SX).reshape(NY, NZ, 16, SX)]

    def y_dot(j, cc):
        rows = G[pl.ds(pl.multiple_of(wrap(y + j, NY) * 128, 128), 128), :]
        return [product(rows, xx, cc, SX, SY).reshape(NZ, 16, SY) for xx in range(NX)]

    def z_dot(j, cc):
        p = product(G[...], j, cc, SX + SY, SZ).reshape(NY, NZ, 16, SZ)
        return [p[:, zz] for zz in range(NZ)]

    def places(part, j):
        if part == "x":
            return [(wrap(x + j, NX),)], (wrap(x + j, NX),)
        if part == "y":
            return [(wrap(y + j, NY), xx) for xx in range(NX)], (wrap(y + j, NY),)
        return [(zz, j) for zz in range(NZ)], (slice(None), j)

    parts = {"x": (x_dot, psx, plx, sx), "y": (y_dot, psy, ply, sy), "z": (z_dot, psz, plz, sz)}
    swaps = {}

    def give(part, j):
        dot, ps, land, _ = parts[part]
        idx, whole = places(part, j)
        for at, p in zip(idx, dot(j, 1 - c)):
            ps[at] = p.astype(BF16)
        swaps[part, j] = remote(ps.at[whole], land.at[whole], dc=1)

    def keep(part, j, extra=None):
        dot, _, land, s = parts[part]
        idx, _ = places(part, j)
        mine = dot(j, c)
        rx(swaps[part, j])
        for at, p in zip(idx, mine):
            s[at] = (p + land[at].astype(F32)).astype(BF16)

    def bump(ref, at, *others):
        total = ref[at].astype(F32)
        for o in others:
            total = total + o.astype(F32)
        ref[at] = total.astype(BF16)

    lo, hi = slice(0, 2), slice(2, 4)

    def send_halves(s, h, me, n, **d):
        (axis,) = d
        far = wrap(me + 2, n)
        return (
            remote(s.at[far, lo], h.at[0], **{axis: 1}),
            remote(s.at[far, hi], h.at[1], **{axis: -1}),
        )

    def near_parts(side):
        return (0, lo, hi) if side == 1 else (1, hi, lo)

    def send_near(s, land, me, n, side, axis):
        at = wrap(me + side, n)
        k, _, alone = near_parts(side)
        return remote(s.at[at, alone], land.at[k, alone], **{axis: side})

    def send_joined(s, h, land, me, n, halves_in, side, axis):
        at = wrap(me + side, n)
        k, joined, _ = near_parts(side)
        rx(halves_in[k])
        for i in (0, 1):
            bump(s, (at, 2 * k + i), h[k, i])
        return remote(s.at[at, joined], land.at[k, joined], **{axis: side})

    give("x", 2)
    give("y", 2)
    for j in range(4):
        give("z", j)
    keep("x", 2)
    xh = send_halves(sx, hx, x, NX, dx=0)
    keep("y", 2)
    yh = send_halves(sy, hy, y, NY, dy=0)
    give("x", 1)
    give("x", 3)
    for j in range(4):
        keep("z", j)

    def zat(k):
        return wrap(z + k, NZ)

    z3r = remote(sz.at[zat(3)], lz3s.at[0], dz=1)
    z3l = remote(sz.at[zat(-3)], lz3s.at[1], dz=-1)
    z4l = remote(sz.at[zat(4), lo], lz4s.at[0], dz=-2)
    z4r = remote(sz.at[zat(4), hi], lz4s.at[1], dz=2)
    z1r = remote(sz.at[zat(1)], lz1.at[0], dz=1)
    z1l = remote(sz.at[zat(-1)], lz1.at[1], dz=-1)
    keep("x", 1)
    x_in = [send_near(sx, lx1, x, NX, 1, "dx")]
    keep("x", 3)
    x_in.append(send_near(sx, lx1, x, NX, -1, "dx"))
    give("y", 1)
    give("y", 3)
    keep("y", 1)
    y_in = [send_near(sy, ly1, y, NY, 1, "dy")]
    keep("y", 3)
    y_in.append(send_near(sy, ly1, y, NY, -1, "dy"))
    give("x", 0)
    give("y", 0)
    for side in (1, -1):
        x_in.append(send_joined(sx, hx, lx1, x, NX, xh, side, "dx"))
    for side in (1, -1):
        y_in.append(send_joined(sy, hy, ly1, y, NY, yh, side, "dy"))
    keep("x", 0)
    keep("y", 0)
    rx(z3r)
    rx(z3l)
    rx(z4l)
    rx(z4r)
    for i in range(NX):
        bump(sz, (zat(-2), i), lz3s[1, i], *([lz4s[0, i]] if i < 2 else []))
    z2l = remote(sz.at[zat(-2)], lz2.at[0], dz=-2)
    for i in range(NX):
        bump(sz, (zat(2), i), lz3s[0, i], *([lz4s[1, i - 2]] if i >= 2 else []))
    z2r = remote(sz.at[zat(2)], lz2.at[1], dz=2)

    far, near = (1 - z // 4) * 4, z // 4 * 4

    def second(s, a, b, n, land, axis):
        return [
            fan(
                [
                    (s.at[a, wrap(b + j, n), pl.ds(h, 4)], land.at[j - 1, pl.ds(h, 4)], {axis: j})
                    for j in (1, 2, 3)
                ],
                land.at[:, pl.ds(h, 4)],
            )
            for h in (far, near)
        ]

    def third(s, a, b, land, out, first):
        h = far if first else near
        bump(s, (a, b, pl.ds(h, 4)), *[land[j, pl.ds(h, 4)] for j in range(3)])
        to = [far + i for i in range(4)] if first else [near + lax.rem(z + k, 4) for k in (1, 2, 3)]
        return fan([(s.at[a, b, zz], out.at[z], dict(to_z=zz)) for zz in to], out.at[0:len(to)])

    for copy in x_in:
        rx(copy)
    for yy in range(NY):
        bump(sx, (x, yy), lx1[0, yy], lx1[1, yy])
    cx = second(sx, x, y, NY, lx2, "dy")
    for copy in y_in:
        rx(copy)
    for xx in range(NX):
        bump(sy, (y, xx), ly1[0, xx], ly1[1, xx])
    cy = second(sy, y, x, NX, ly2, "dx")
    weight_grad(0, 2)
    for copy in (z1r, z1l, z2l, z2r):
        rx(copy)
    for xx in range(NX):
        bump(sz, (z, xx), lz1[0, xx], lz1[1, xx], lz2[0, xx], lz2[1, xx])
    cz = fan([(sz.at[z, wrap(x + j, NX)], lz5.at[j - 1], dict(dx=j)) for j in (1, 2, 3)], lz5)

    rx(cx[0])
    cx[0] = third(sx, x, y, lx2, lx3, True)
    rx(cy[0])
    cy[0] = third(sy, y, x, ly2, ly3, True)
    rx(cx[1])
    cx[1] = third(sx, x, y, lx2, lx3, False)
    rx(cy[1])
    cy[1] = third(sy, y, x, ly2, ly3, False)
    rx(cz)
    bump(sz, (z, x), lz5[0], lz5[1], lz5[2])
    cz = fan([(sz.at[z, x, wrap(y + j, NY)], lz3.at[j - 1], dict(dy=j)) for j in (1, 2, 3)], lz3)
    weight_grad(2, 4)
    drain()
    rx(cx[0])
    rx(cx[1])
    total = sx[x, y, z].astype(F32)
    for k in range(1, NZ):
        total = total + lx3[zat(k)].astype(F32)
    dh_ref[:, 0:SX] = total.astype(BF16)
    rx(cy[0])
    rx(cy[1])
    total = sy[y, x, z].astype(F32)
    for k in range(1, NZ):
        total = total + ly3[zat(k)].astype(F32)
    dh_ref[:, SX:SX + SY] = total.astype(BF16)
    rx(cz)
    total = sz[z, x, y].astype(F32)
    for k in range(3):
        total = total + lz3[k].astype(F32)
    dh_ref[:, SX + SY:] = total.astype(BF16)


def run_kernel(hidden, weight, targets, row_seq, ref_logp):
    vmem = pl.BlockSpec(memory_space=pltpu.VMEM)
    hbm = pl.BlockSpec(memory_space=pl.ANY)

    def v16(*shape):
        return pltpu.VMEM(shape, BF16)

    chunks = [v16(NX, NY, NZ, 16, SX), v16(NY, NX, NZ, 16, SY), v16(NZ, NX, NY, 16, SZ)]
    return pl.pallas_call(
        fused_kernel,
        out_shape=(
            pltpu.VMEM((D, VSH), BF16),
            pltpu.VMEM((8, 128), F32),
            pltpu.VMEM((16, 1024), BF16),
        ),
        in_specs=[hbm] * 5,
        out_specs=(vmem, vmem, vmem),
        scratch_shapes=[
            v16(NY, NZ, 16, D),
            v16(D, VSH),
            pltpu.VMEM((NY, NZ, 16, VSH), F32),
            pltpu.VMEM((VSH, ROWS), F32),
            v16(ROWS, VSH),
            pltpu.VMEM((3, 8, 128), F32),
            pltpu.VMEM((8, 128), F32),
            pltpu.VMEM((15, 8, 128), F32),
            pltpu.VMEM((7, 8, 128), F32),
            *chunks, *chunks, *chunks,
            v16(2, 2, NZ, 16, SX), v16(2, NY, NZ, 16, SX), v16(3, NZ, 16, SX), v16(NZ, 16, SX),
            v16(2, 2, NZ, 16, SY), v16(2, NX, NZ, 16, SY), v16(3, NZ, 16, SY), v16(NZ, 16, SY),
            v16(2, NX, NY, 16, SZ), v16(2, 2, NY, 16, SZ), v16(2, NX, NY, 16, SZ),
            v16(2, NX, NY, 16, SZ), v16(3, NY, 16, SZ), v16(3, 16, SZ),
            pltpu.VMEM((4, 128), jnp.int32), pltpu.VMEM((4, 128), jnp.int32), pltpu.VMEM((1, 2), F32),
            pltpu.SemaphoreType.DMA((6,)),
            pltpu.SemaphoreType.DMA((N_SEM,)),
            pltpu.SemaphoreType.DMA((N_SEM,)),
        ],
        compiler_params=pltpu.CompilerParams(
            collective_id=0, has_side_effects=True, vmem_limit_bytes=52 * 2**20
        ),
        cost_estimate=pl.CostEstimate(flops=2 * 2 * ROWS * D * VSH, bytes_accessed=2 * D * VSH, transcendentals=0),
    )(hidden, weight, targets.reshape(4, 128), row_seq.reshape(4, 128), ref_logp.reshape(1, 2))


def on_device(hidden, weight, targets, row_seq, ref_logp):
    dw, loss, dh = run_kernel(hidden, weight, targets, row_seq, ref_logp)

    def leave(dw_ref, loss_ref, dh_ref, dw_out, loss_out, dh_out, sem):
        copy = pltpu.make_async_copy(dw_ref, dw_out, sem.at[0])
        copy.start()
        loss_out[0] = loss_ref[0, 0]
        dh_out[...] = dh_ref[...]
        copy.wait()

    vmem = pl.BlockSpec(memory_space=pltpu.VMEM)
    d_weight, dpo_loss, d_hidden = pl.pallas_call(
        leave,
        out_shape=(
            jax.ShapeDtypeStruct((D, VSH), BF16),
            jax.ShapeDtypeStruct((1,), F32),
            jax.ShapeDtypeStruct((16, 1024), BF16),
        ),
        in_specs=[vmem, vmem, vmem],
        out_specs=(pl.BlockSpec(memory_space=pl.ANY), pl.BlockSpec(memory_space=pltpu.SMEM), vmem),
        scratch_shapes=[pltpu.SemaphoreType.DMA((1,))],
        compiler_params=pltpu.CompilerParams(has_side_effects=True, vmem_limit_bytes=16 * 2**20),
    )(dw, loss, dh)
    return (dpo_loss[0], d_hidden, d_weight)


def solution(mesh):
    placed = (P("ctx", None), P(None, ("ctx", "tp")), P(), P(), P())
    return jax.shard_map(
        on_device,
        mesh=mesh,
        in_specs=placed,
        out_specs=(P(), P("ctx", "tp"), P(None, ("ctx", "tp"))),
        check_vma=False,
    )
```

```python
import functools

import jax
import jax.numpy as jnp
from jax import lax
from jax.experimental import pallas as pl
from jax.experimental.pallas import tpu as pltpu
from jax.sharding import PartitionSpec as P

MESH = pl.DeviceIdType.MESH
F32 = jnp.float32
BF16 = jnp.bfloat16

DPO_BETA = 0.01
LOSS_SCALE = 1024.0

NX, NY, NZ = 4, 4, 8
ROWS = 512
D = 8192
VSH = 384
HALF = 4096

GA, GB, GQ = 1024, 1536, 384
SX, SY, SZ = 384, 384, 256

N_SEM = 53

KC = 1024


def fused_kernel(
    hid_ref, w_ref, tgt_in, seq_in, ref_in,
    dw_ref, loss_ref, dh_ref,
    H, W, L, logits_t, G,
    st_own, st_core, st_xy, st_z,
    psx, psy, psz, plx, ply, plz, sx, sy, sz,
    hx, lx1, lx2, lx3, hy, ly1, ly2, ly3, lz3s, lz4s, lz1, lz2, lz5, lz3,
    tgt_ref, seq_ref, ref_ref, local_sem, ssem, rsem,
):
    ctx = lax.axis_index("ctx")
    tp = lax.axis_index("tp")
    y = ctx // NZ
    z = lax.rem(ctx, NZ)
    x = tp // 2
    c = lax.rem(tp, 2)

    def wrap(v, n):
        return lax.rem(v + n, n)

    def dev(dy=0, dz=0, dx=0, dc=0, to_z=None):
        yy = wrap(y + dy, NY) if dy else y
        zz = wrap(z + dz, NZ) if dz else z
        zz = zz if to_z is None else to_z
        xx = wrap(x + dx, NX) if dx else x
        cc = 1 - c if dc else c
        return (yy * NZ + zz, xx * 2 + cc)

    counter = [0]
    sends = []

    def number():
        counter[0] += 1
        return counter[0] - 1

    def remote(src, dst, i=None, **d):
        i_own = number() if i is None else i
        copy = pltpu.make_async_remote_copy(
            src_ref=src, dst_ref=dst, send_sem=ssem.at[i_own], recv_sem=rsem.at[i_own],
            device_id=dev(**d), device_id_type=MESH,
        )
        copy.start()
        if i is None:
            sends.append(copy)
            return copy

    def all_of(i, whole, **d):
        copy = pltpu.make_async_remote_copy(
            src_ref=whole, dst_ref=whole, send_sem=ssem.at[i], recv_sem=rsem.at[i],
            device_id=dev(**d), device_id_type=MESH,
        )
        sends.append(copy)
        return copy

    def fan(pairs, whole):
        i = number()
        for src, dst, d in pairs:
            remote(src, dst, i, **d)
        return all_of(i, whole, **pairs[0][2])

    def rx(copy):
        copy.wait_recv()

    def drain():
        for copy in sends:
            copy.wait_send()
        sends.clear()

    c0 = c * HALF
    col_a = pl.multiple_of(c0, 128)
    col_b = pl.multiple_of(c0 + GA, 128)
    col_q0 = pl.multiple_of(c0 + GA + GB, 128)
    col_q = pl.multiple_of(c0 + GA + GB + x * GQ, 128)

    w_load = pltpu.make_async_copy(w_ref, W, local_sem.at[0])
    w_load.start()
    own_ab = pltpu.make_async_copy(
        hid_ref.at[:, pl.ds(col_a, GA + GB)], H.at[y, z, :, pl.ds(col_a, GA + GB)], local_sem.at[1]
    )
    own_ab.start()
    own_q = pltpu.make_async_copy(
        hid_ref.at[:, pl.ds(col_q, GQ)], H.at[y, z, :, pl.ds(col_q, GQ)], local_sem.at[2]
    )
    own_q.start()

    small = [
        pltpu.make_async_copy(src, dst, local_sem.at[3 + n])
        for n, (src, dst) in enumerate(((tgt_in, tgt_ref), (seq_in, seq_ref), (ref_in, ref_ref)))
    ]
    for copy in small:
        copy.start()

    barrier = pltpu.get_barrier_semaphore()
    plane = [(i, j) for i in range(NX) for j in range(NY) if i or j]
    plane.sort(key=lambda p: -min(p[0], NX - p[0]) - min(p[1], NY - p[1]))
    line = sorted(range(1, NZ), key=lambda k: -min(k, NZ - k))
    peers = [dict(dx=i, dy=j) for i, j in plane] + [dict(dz=k) for k in line] + [dict(dc=1)]
    for p in peers:
        pl.semaphore_signal(barrier, inc=1, device_id=dev(**p), device_id_type=MESH)
    pl.semaphore_wait(barrier, len(peers))
    for copy in small:
        copy.wait()
    own_ab.wait()
    own_q.wait()

    def blk_a(zz):
        return H.at[:, zz, :, pl.ds(col_a, GA)]

    def blk_b(yy, zz):
        return H.at[yy, zz, :, pl.ds(col_b, GB)]

    def blk_q(zz):
        return H.at[:, zz, :, pl.ds(col_q, GQ)]

    own_a = H.at[y, z, :, pl.ds(col_a, GA)]
    own_qb = H.at[y, z, :, pl.ds(col_q, GQ)]
    first_a = fan([(own_a, own_a, dict(dy=j)) for j in (1, 2, 3)], H.at[0:3, z, :, pl.ds(col_a, GA)])
    first_q = fan([(own_qb, own_qb, dict(dy=j)) for j in (1, 2, 3)], H.at[0:3, z, :, pl.ds(col_q, GQ)])

    def both_ways(ref):
        return (remote(ref, ref, dz=1), remote(ref, ref, dz=-1))

    def fan_y(zz):
        ref = blk_b(y, zz)
        return fan([(ref, ref, dict(dy=j)) for j in (1, 2, 3)], H.at[0:3, zz, :, pl.ds(col_b, GB)])

    def fan_x(zz):
        ref = blk_q(zz)
        return fan([(ref, ref, dict(dx=j)) for j in (1, 2, 3)], H.at[:, zz, :, pl.ds(col_q0, 3 * GQ)])

    handed = {}
    arrivals = {}

    def hand_over(key, ref):
        if key not in handed:
            handed[key] = number()
        remote(ref, ref, handed[key], dc=1)

    def hand_on(key, zz):
        from_y, from_x = arrivals.pop(key)
        rx(from_y)
        hand_over(key, H.at[:, zz, :, pl.ds(col_b, GB)])
        rx(from_x)
        hand_over(key, H.at[:, zz, :, pl.ds(col_q0, NX * GQ)])
        handed[key] = all_of(handed[key], H.at[:, zz, :, pl.ds(col_a, HALF)], dc=1)

    def logits_of(keys):
        zs = [wrap(z - sign * st, NZ) for st, sign in keys]
        for key in keys:
            rx(handed[key])
        acc = jnp.zeros((64 * len(zs), VSH), F32)
        for k in range(0, D, KC):
            h = jnp.concatenate([H[yy, zz, :, k:k + KC] for zz in zs for yy in range(NY)], axis=0)
            acc = acc + jnp.dot(h, W[k:k + KC, :], preferred_element_type=F32)
        acc = acc.reshape(len(zs), NY, 16, VSH)
        for n, zz in enumerate(zs):
            L[:, zz] = acc[n]

    ring_b = both_ways(blk_b(y, z))
    fy = fan_y(z)
    rx(first_a)
    ring_a = both_ways(blk_a(z))
    rx(first_q)
    ring_q = both_ways(blk_q(z))
    fx = fan_x(z)
    hand_over((0, 1), blk_a(z))
    arrivals[0, 1] = (fy, fx)

    def halves(yy, zz, col, n, k):
        cut = n // 256 * 128
        lo = col if k == 0 else pl.multiple_of(col + cut, 128)
        return H.at[yy, zz, :, pl.ds(lo, cut if k == 0 else n - cut)]

    for s in (1, 2, 3):
        nb, na, nq = [], [], []
        for k, sign in ((0, 1), (1, -1)):
            zz = wrap(z - sign * s, NZ)
            rx(ring_b[k])
            ref = blk_b(y, zz) if s < 3 else halves(y, zz, col_b, GB, k)
            nb.append(remote(ref, ref, dz=sign))
            fy = fan_y(zz)
            rx(ring_q[k])
            ref = blk_q(zz) if s < 3 else halves(slice(None), zz, col_q, GQ, k)
            nq.append(remote(ref, ref, dz=sign))
            fx = fan_x(zz)
            rx(ring_a[k])
            ref = blk_a(zz) if s < 3 else halves(slice(None), zz, col_a, GA, k)
            na.append(remote(ref, ref, dz=sign))
            hand_over((s, sign), blk_a(zz))
            arrivals[s, sign] = (fy, fx)
        for key in list(arrivals):
            if key[0] < s:
                hand_on(key, wrap(z - key[1] * key[0], NZ))
        if s == 2:
            w_load.wait()
        if s == 3:
            logits_of([(1, 1), (1, -1)])
        ring_b, ring_a, ring_q = nb, na, nq

    zz = wrap(z + 4, NZ)
    rx(ring_b[0])
    rx(ring_b[1])
    fy = fan_y(zz)
    rx(ring_q[0])
    rx(ring_q[1])
    fx = fan_x(zz)
    rx(ring_a[0])
    rx(ring_a[1])
    hand_over((4, -1), blk_a(zz))
    arrivals[4, -1] = (fy, fx)
    hand_on((3, 1), wrap(z - 3, NZ))
    hand_on((3, -1), wrap(z + 3, NZ))
    logits_of([(2, 1), (2, -1)])
    hand_on((4, -1), zz)
    logits_of([(3, 1), (3, -1)])
    logits_of([(0, 1), (4, -1)])

    lt = L[...].reshape(ROWS, VSH).T
    logits_t[...] = lt

    def lanes(ref4):
        return jnp.concatenate([ref4[i:i + 1, :] for i in range(4)], axis=1)

    targets = lanes(tgt_ref[...])
    first_col = (ctx * 8 + tp) * VSH
    cols = first_col + lax.broadcasted_iota(jnp.int32, (VSH, ROWS), 0)
    matches = cols == targets
    peak = jnp.max(lt, axis=0, keepdims=True)
    local_lse = peak + jnp.log(jnp.sum(jnp.exp(lt - peak), axis=0, keepdims=True))
    picked = jnp.sum(jnp.where(matches, lt, 0.0), axis=0, keepdims=True)
    for i in range(4):
        st_own[0, i:i + 1, :] = local_lse[:, i * 128:(i + 1) * 128]
        st_own[0, 4 + i:5 + i, :] = picked[:, i * 128:(i + 1) * 128]

    def merge(mine, others):
        every = [mine] + others
        top = functools.reduce(jnp.maximum, every)
        total = functools.reduce(jnp.add, [jnp.exp(e - top) for e in every])
        summed = functools.reduce(jnp.add, every)
        row = lax.broadcasted_iota(jnp.int32, (8, 128), 0)
        return jnp.where(row < 4, top + jnp.log(total), summed)

    copy = remote(st_own.at[0], st_core, dc=1)
    rx(copy)
    st = merge(st_own[0], [st_core[...]])
    st_own[1] = st
    gathered = sends[:]
    sends.clear()
    copy = fan([(st_own.at[1], st_xy.at[n], dict(dx=i, dy=j)) for n, (i, j) in enumerate(plane)], st_xy)
    for earlier in gathered:
        earlier.wait_send()
    rx(copy)
    st = merge(st, [st_xy[n] for n in range(15)])
    st_own[2] = st
    rx(fan([(st_own.at[2], st_z.at[n], dict(dz=k)) for n, k in enumerate(line)], st_z))
    drain()
    counter[0] = 0
    st = merge(st, [st_z[n] for n in range(7)])
    lse4 = st[0:4, :]
    logp4 = st[4:8, :] - lse4
    seq4 = seq_ref[...]

    def total_of(v):
        return jnp.sum(jnp.sum(v, axis=1, keepdims=True), axis=0, keepdims=True)

    seq0 = total_of(jnp.where(seq4 == 0, logp4, 0.0))
    seq1 = total_of(jnp.where(seq4 == 1, logp4, 0.0))
    margin = DPO_BETA * ((seq0 - ref_ref[:, 0:1]) - (seq1 - ref_ref[:, 1:2]))
    neg = jnp.broadcast_to(-margin, (8, 128))
    loss_ref[...] = jnp.maximum(neg, 0.0) + jnp.log1p(jnp.exp(-jnp.abs(neg)))
    pull = (LOSS_SCALE * DPO_BETA) / (1.0 + jnp.exp(margin))
    coef4 = jnp.where(seq4 == 0, -pull, jnp.where(seq4 == 1, pull, 0.0))
    lse = lanes(lse4)
    coef = lanes(coef4)
    lt = logits_t[...]
    g_t = coef * (matches.astype(F32) - jnp.exp(lt - lse))
    g = g_t.T.astype(BF16)
    G[...] = g

    def weight_grad(first, last):
        n = 512

        def step(i, carry):
            for k in range(4):
                at = pl.ds(pl.multiple_of(i * 4 * n + k * n, n), n)
                h = H[:, :, :, at].reshape(ROWS, n)
                dw_ref[at, :] = lax.dot_general(
                    h, G[...], (((0,), (0,)), ((), ())), preferred_element_type=F32
                ).astype(BF16)
            return carry

        lax.fori_loop(first, last, step, 0)

    def product(rows, xx, cc, off, n):
        start = pl.multiple_of((xx * 2 + cc) * 1024 + off, 128)
        return lax.dot_general(
            rows, W[pl.ds(start, n), :], (((1,), (1,)), ((), ())), preferred_element_type=F32
        )

    def x_dot(j, cc):
        return [product(G[...], wrap(x + j, NX), cc, 0, SX).reshape(NY, NZ, 16, SX)]

    def y_dot(j, cc):
        rows = G[pl.ds(pl.multiple_of(wrap(y + j, NY) * 128, 128), 128), :]
        return [product(rows, xx, cc, SX, SY).reshape(NZ, 16, SY) for xx in range(NX)]

    def z_dot(j, cc):
        p = product(G[...], j, cc, SX + SY, SZ).reshape(NY, NZ, 16, SZ)
        return [p[:, zz] for zz in range(NZ)]

    def places(part, j):
        if part == "x":
            return [(wrap(x + j, NX),)], (wrap(x + j, NX),)
        if part == "y":
            return [(wrap(y + j, NY), xx) for xx in range(NX)], (wrap(y + j, NY),)
        return [(zz, j) for zz in range(NZ)], (slice(None), j)

    parts = {"x": (x_dot, psx, plx, sx), "y": (y_dot, psy, ply, sy), "z": (z_dot, psz, plz, sz)}
    swaps = {}

    def give(part, j):
        dot, ps, land, _ = parts[part]
        idx, whole = places(part, j)
        for at, p in zip(idx, dot(j, 1 - c)):
            ps[at] = p.astype(BF16)
        swaps[part, j] = remote(ps.at[whole], land.at[whole], dc=1)

    def keep(part, j, extra=None):
        dot, _, land, s = parts[part]
        idx, _ = places(part, j)
        mine = dot(j, c)
        rx(swaps[part, j])
        for at, p in zip(idx, mine):
            s[at] = (p + land[at].astype(F32)).astype(BF16)

    def bump(ref, at, *others):
        total = ref[at].astype(F32)
        for o in others:
            total = total + o.astype(F32)
        ref[at] = total.astype(BF16)

    lo, hi = slice(0, 2), slice(2, 4)

    def send_halves(s, h, me, n, **d):
        (axis,) = d
        far = wrap(me + 2, n)
        return (
            remote(s.at[far, lo], h.at[0], **{axis: 1}),
            remote(s.at[far, hi], h.at[1], **{axis: -1}),
        )

    def near_parts(side):
        return (0, lo, hi) if side == 1 else (1, hi, lo)

    def send_near(s, land, me, n, side, axis):
        at = wrap(me + side, n)
        k, _, alone = near_parts(side)
        return remote(s.at[at, alone], land.at[k, alone], **{axis: side})

    def send_joined(s, h, land, me, n, halves_in, side, axis):
        at = wrap(me + side, n)
        k, joined, _ = near_parts(side)
        rx(halves_in[k])
        for i in (0, 1):
            bump(s, (at, 2 * k + i), h[k, i])
        return remote(s.at[at, joined], land.at[k, joined], **{axis: side})

    give("x", 2)
    give("y", 2)
    give("x", 1)
    give("x", 3)
    for j in range(4):
        give("z", j)
    keep("x", 2)
    xh = send_halves(sx, hx, x, NX, dx=0)
    keep("y", 2)
    yh = send_halves(sy, hy, y, NY, dy=0)
    for j in range(4):
        keep("z", j)

    def zat(k):
        return wrap(z + k, NZ)

    z3r = remote(sz.at[zat(3)], lz3s.at[0], dz=1)
    z3l = remote(sz.at[zat(-3)], lz3s.at[1], dz=-1)
    z4l = remote(sz.at[zat(4), lo], lz4s.at[0], dz=-2)
    z4r = remote(sz.at[zat(4), hi], lz4s.at[1], dz=2)
    z1r = remote(sz.at[zat(1)], lz1.at[0], dz=1)
    z1l = remote(sz.at[zat(-1)], lz1.at[1], dz=-1)
    keep("x", 1)
    x_in = [send_near(sx, lx1, x, NX, 1, "dx")]
    keep("x", 3)
    x_in.append(send_near(sx, lx1, x, NX, -1, "dx"))
    give("y", 1)
    give("y", 3)
    keep("y", 1)
    y_in = [send_near(sy, ly1, y, NY, 1, "dy")]
    keep("y", 3)
    y_in.append(send_near(sy, ly1, y, NY, -1, "dy"))
    give("x", 0)
    give("y", 0)
    for side in (1, -1):
        x_in.append(send_joined(sx, hx, lx1, x, NX, xh, side, "dx"))
    for side in (1, -1):
        y_in.append(send_joined(sy, hy, ly1, y, NY, yh, side, "dy"))
    keep("x", 0)
    keep("y", 0)
    rx(z3r)
    rx(z3l)
    rx(z4l)
    rx(z4r)
    for i in range(NX):
        bump(sz, (zat(-2), i), lz3s[1, i], *([lz4s[0, i]] if i < 2 else []))
    z2l = remote(sz.at[zat(-2)], lz2.at[0], dz=-2)
    for i in range(NX):
        bump(sz, (zat(2), i), lz3s[0, i], *([lz4s[1, i - 2]] if i >= 2 else []))
    z2r = remote(sz.at[zat(2)], lz2.at[1], dz=2)

    far, near = (1 - z // 4) * 4, z // 4 * 4

    def second(s, a, b, n, land, axis):
        return [
            fan(
                [
                    (s.at[a, wrap(b + j, n), pl.ds(h, 4)], land.at[j - 1, pl.ds(h, 4)], {axis: j})
                    for j in (1, 2, 3)
                ],
                land.at[:, pl.ds(h, 4)],
            )
            for h in (far, near)
        ]

    def third(s, a, b, land, out, first):
        h = far if first else near
        bump(s, (a, b, pl.ds(h, 4)), *[land[j, pl.ds(h, 4)] for j in range(3)])
        to = [far + i for i in range(4)] if first else [near + lax.rem(z + k, 4) for k in (1, 2, 3)]
        return fan([(s.at[a, b, zz], out.at[z], dict(to_z=zz)) for zz in to], out.at[0:len(to)])

    for copy in x_in:
        rx(copy)
    for yy in range(NY):
        bump(sx, (x, yy), lx1[0, yy], lx1[1, yy])
    cx = second(sx, x, y, NY, lx2, "dy")
    for copy in y_in:
        rx(copy)
    for xx in range(NX):
        bump(sy, (y, xx), ly1[0, xx], ly1[1, xx])
    cy = second(sy, y, x, NX, ly2, "dx")
    weight_grad(0, 2)
    for copy in (z1r, z1l, z2l, z2r):
        rx(copy)
    for xx in range(NX):
        bump(sz, (z, xx), lz1[0, xx], lz1[1, xx], lz2[0, xx], lz2[1, xx])
    cz = fan([(sz.at[z, wrap(x + j, NX)], lz5.at[j - 1], dict(dx=j)) for j in (1, 2, 3)], lz5)

    rx(cx[0])
    cx[0] = third(sx, x, y, lx2, lx3, True)
    rx(cy[0])
    cy[0] = third(sy, y, x, ly2, ly3, True)
    rx(cx[1])
    cx[1] = third(sx, x, y, lx2, lx3, False)
    rx(cy[1])
    cy[1] = third(sy, y, x, ly2, ly3, False)
    rx(cz)
    bump(sz, (z, x), lz5[0], lz5[1], lz5[2])
    cz = fan([(sz.at[z, x, wrap(y + j, NY)], lz3.at[j - 1], dict(dy=j)) for j in (1, 2, 3)], lz3)
    weight_grad(2, 4)
    drain()
    rx(cx[0])
    rx(cx[1])
    total = sx[x, y, z].astype(F32)
    for k in range(1, NZ):
        total = total + lx3[zat(k)].astype(F32)
    dh_ref[:, 0:SX] = total.astype(BF16)
    rx(cy[0])
    rx(cy[1])
    total = sy[y, x, z].astype(F32)
    for k in range(1, NZ):
        total = total + ly3[zat(k)].astype(F32)
    dh_ref[:, SX:SX + SY] = total.astype(BF16)
    rx(cz)
    total = sz[z, x, y].astype(F32)
    for k in range(3):
        total = total + lz3[k].astype(F32)
    dh_ref[:, SX + SY:] = total.astype(BF16)


def run_kernel(hidden, weight, targets, row_seq, ref_logp):
    vmem = pl.BlockSpec(memory_space=pltpu.VMEM)
    hbm = pl.BlockSpec(memory_space=pl.ANY)

    def v16(*shape):
        return pltpu.VMEM(shape, BF16)

    chunks = [v16(NX, NY, NZ, 16, SX), v16(NY, NX, NZ, 16, SY), v16(NZ, NX, NY, 16, SZ)]
    return pl.pallas_call(
        fused_kernel,
        out_shape=(
            pltpu.VMEM((D, VSH), BF16),
            pltpu.VMEM((8, 128), F32),
            pltpu.VMEM((16, 1024), BF16),
        ),
        in_specs=[hbm] * 5,
        out_specs=(vmem, vmem, vmem),
        scratch_shapes=[
            v16(NY, NZ, 16, D),
            v16(D, VSH),
            pltpu.VMEM((NY, NZ, 16, VSH), F32),
            pltpu.VMEM((VSH, ROWS), F32),
            v16(ROWS, VSH),
            pltpu.VMEM((3, 8, 128), F32),
            pltpu.VMEM((8, 128), F32),
            pltpu.VMEM((15, 8, 128), F32),
            pltpu.VMEM((7, 8, 128), F32),
            *chunks, *chunks, *chunks,
            v16(2, 2, NZ, 16, SX), v16(2, NY, NZ, 16, SX), v16(3, NZ, 16, SX), v16(NZ, 16, SX),
            v16(2, 2, NZ, 16, SY), v16(2, NX, NZ, 16, SY), v16(3, NZ, 16, SY), v16(NZ, 16, SY),
            v16(2, NX, NY, 16, SZ), v16(2, 2, NY, 16, SZ), v16(2, NX, NY, 16, SZ),
            v16(2, NX, NY, 16, SZ), v16(3, NY, 16, SZ), v16(3, 16, SZ),
            pltpu.VMEM((4, 128), jnp.int32), pltpu.VMEM((4, 128), jnp.int32), pltpu.VMEM((1, 2), F32),
            pltpu.SemaphoreType.DMA((6,)),
            pltpu.SemaphoreType.DMA((N_SEM,)),
            pltpu.SemaphoreType.DMA((N_SEM,)),
        ],
        compiler_params=pltpu.CompilerParams(
            collective_id=0, has_side_effects=True, vmem_limit_bytes=52 * 2**20
        ),
        cost_estimate=pl.CostEstimate(flops=2 * 2 * ROWS * D * VSH, bytes_accessed=2 * D * VSH, transcendentals=0),
    )(hidden, weight, targets.reshape(4, 128), row_seq.reshape(4, 128), ref_logp.reshape(1, 2))


def on_device(hidden, weight, targets, row_seq, ref_logp):
    dw, loss, dh = run_kernel(hidden, weight, targets, row_seq, ref_logp)

    def leave(dw_ref, loss_ref, dh_ref, dw_out, loss_out, dh_out, sem):
        copy = pltpu.make_async_copy(dw_ref, dw_out, sem.at[0])
        copy.start()
        loss_out[0] = loss_ref[0, 0]
        dh_out[...] = dh_ref[...]
        copy.wait()

    vmem = pl.BlockSpec(memory_space=pltpu.VMEM)
    d_weight, dpo_loss, d_hidden = pl.pallas_call(
        leave,
        out_shape=(
            jax.ShapeDtypeStruct((D, VSH), BF16),
            jax.ShapeDtypeStruct((1,), F32),
            jax.ShapeDtypeStruct((16, 1024), BF16),
        ),
        in_specs=[vmem, vmem, vmem],
        out_specs=(pl.BlockSpec(memory_space=pl.ANY), pl.BlockSpec(memory_space=pltpu.SMEM), vmem),
        scratch_shapes=[pltpu.SemaphoreType.DMA((1,))],
        compiler_params=pltpu.CompilerParams(has_side_effects=True, vmem_limit_bytes=16 * 2**20),
    )(dw, loss, dh)
    return (dpo_loss[0], d_hidden, d_weight)


def solution(mesh):
    placed = (P("ctx", None), P(None, ("ctx", "tp")), P(), P(), P())
    return jax.shard_map(
        on_device,
        mesh=mesh,
        in_specs=placed,
        out_specs=(P(), P("ctx", "tp"), P(None, ("ctx", "tp"))),
        check_vma=False,
    )
```
